128 devices in a mesh: dp: 8 (over x, core), expert: 16 (over y, z).
Axes of the slice: x: 4, y: 4, z: 4, core: 2. Of those that a mesh axis runs over, the one named last changes fastest.
Arguments:
- tokens: bfloat16 [20480, 4096], P(('dp', 'expert')), may hold values from -6 to 6
- gate_probs: float32 [20480, 2], P(('dp', 'expert')), may hold values from 0.2 to 1
- expert_ids: int32 [20480, 2], P(('dp', 'expert')), may hold values from 0 to 15, all different within a row
- placement: int32 [16, 8], replicated, may hold values from 0 to 7, as said below
- replica: int32 [20480, 2], P(('dp', 'expert')), may hold values from 0 to 7
- row_counts: int32 [128], P(('dp', 'expert')), may hold values from 120 to 160
- w_gate: bfloat16 [16, 4096, 768], P('expert'), may hold values from -0.09375 to 0.09375
- w_up: bfloat16 [16, 4096, 768], P('expert'), may hold values from -0.09375 to 0.09375
- w_down: bfloat16 [16, 768, 4096], P('expert'), may hold values from -0.21875 to 0.21875
- d_out: bfloat16 [20480, 4096], P(('dp', 'expert')), may hold values from -6 to 6
Outputs:
- layer_out: bfloat16 [20480, 4096], P(('dp', 'expert'))
- d_tokens: bfloat16 [20480, 4096], P(('dp', 'expert'))
- d_gates: float32 [20480, 2], P(('dp', 'expert'))
- g_gate: bfloat16 [16, 4096, 768], P('expert', 'dp')
- g_up: bfloat16 [16, 4096, 768], P('expert', 'dp')
- g_down: bfloat16 [16, 768, 4096], P('expert', None, 'dp')
The draws below stay inside these ranges and needn't reach their ends.
Inputs may be any that keep to these rules, and one draw needn't show every extreme that they name: `placement`: each expert's list names 1 to 8 distinct dp indices, repeated in order; in every draw some expert's list names all of them.
All inputs are finite; a program needn't handle non-finite values.
Results may differ from the reference program's by a relative error of at most 0.015.
Values may be sent and summed in bfloat16 or wider, within the bound.
A program may use at most 192 MiB of HBM per device.

```python
import jax
import jax.numpy as jnp
from jax import lax

D = 4096
F = 768
TOK_DEV = 160
TOP_COUNT = 2
E = 16
CAP = 2
TOKENS = 20480
N_DP = 8
N_EXPERT = 16
DEVICES = 128


def draw_placement(key, part):
    key = jax.random.fold_in(key, 7)
    key_count, key_full, key_perm = jax.random.split(key, 3)
    levels = N_DP.bit_length()
    powers = jax.random.randint(key_count, (E,), 0, levels)
    full_one = jax.random.randint(key_full, (), 0, E)
    holders = jnp.minimum(jnp.left_shift(jnp.ones_like(powers), powers), N_DP)
    holders = jnp.where(jnp.arange(E) == full_one, N_DP, holders)
    orders = jax.vmap(lambda sub_key: jax.random.permutation(sub_key, N_DP))(jax.random.split(key_perm, E))
    column = jnp.arange(N_DP)[None, :] % holders[:, None]
    return jnp.take_along_axis(orders, column, axis=1).astype(jnp.int32)


def with_ends(values, stream_key, least, largest):
    longest = values.shape.index(max(values.shape))
    spots = []
    for shift in (0, 1):
        where = [jax.random.randint(jax.random.fold_in(stream_key, axis), (), 0, length) for axis, length in enumerate(values.shape)]
        where[longest] = (where[longest] + shift) % values.shape[longest]
        spots.append(tuple(where))
    return values.at[spots[0]].set(least).at[spots[1]].set(largest)


def block_scale(own_key, extent, pieces, least, top_value):
    loudness = 1.0
    for position, blocks in pieces:
        heights = jax.random.uniform(jax.random.fold_in(jax.random.fold_in(own_key, 6), position), (blocks,), jnp.float32, least / len(pieces), top_value / len(pieces))
        loudness = loudness * jnp.repeat(jnp.exp(heights), extent[position] // blocks).reshape((-1,) + (1,) * (len(extent) - 1 - position))
    return loudness


def different_ones(own_key, rows, number_of, top, lift):
    order = jax.random.permutation(jax.random.fold_in(own_key, 1), number_of)
    pull = order
    for power in range(3):
        pull = pull * pull // number_of
    pull = pull * lift // number_of
    chance = jax.random.randint(jax.random.fold_in(own_key, 2), (rows, number_of), 0, 4096) + pull
    sure = jax.random.permutation(jax.random.fold_in(own_key, 3), rows)[jnp.arange(number_of) % rows]
    chance = jnp.where(jnp.arange(rows)[:, None] == sure[None, :], 1 << 14, chance)
    priority = chance * number_of + jnp.arange(number_of)
    return lax.top_k(priority.astype(jnp.int32), top)[1].astype(jnp.int32)


def scatter_about(rng, shape, spread, bound, cuts=(), kind=jnp.bfloat16):
    gain = block_scale(rng, shape, cuts, -0.22, 0.18) if cuts else 1.0
    array = jax.random.normal(rng, shape, jnp.float32) * spread * gain
    return jnp.minimum(jnp.maximum(array, -bound), bound).astype(kind)


def setup_inputs(seed: int = 0) -> dict:
    seeds = jax.random.split(jax.random.key(seed), 11)
    tokens = scatter_about(seeds[0], (TOKENS, D), 1.0, 6.0, ((0, 128),))
    gate_probs = jnp.clip(0.2 + 0.8 * jax.random.uniform(seeds[1], (TOKENS, TOP_COUNT), jnp.float32) ** block_scale(seeds[1], (TOKENS, TOP_COUNT), ((0, 128),), -0.2, 0.2), 0.2, 1.0)
    expert_ids = different_ones(seeds[2], TOKENS, E, TOP_COUNT, 2048)
    placement = draw_placement(jax.random.fold_in(seeds[10], 71), 0)
    replica = with_ends(jax.random.randint(seeds[4], (TOKENS, TOP_COUNT), 0, N_DP), jax.random.fold_in(seeds[4], 1), 0, N_DP - 1).astype(jnp.int32)
    row_counts = with_ends(jax.random.randint(seeds[5], (DEVICES,), 3 * TOK_DEV // 4, TOK_DEV + 1), jax.random.fold_in(seeds[5], 1), 3 * TOK_DEV // 4, TOK_DEV).astype(jnp.int32)
    w_gate = scatter_about(seeds[6], (E, D, F), D ** -0.5, 0.09375, ((0, 16),))
    w_up = scatter_about(seeds[7], (E, D, F), D ** -0.5, 0.09375, ((0, 16),))
    w_down = scatter_about(seeds[8], (E, F, D), F ** -0.5, 0.21875, ((0, 16),))
    d_out = scatter_about(seeds[9], (TOKENS, D), 1.0, 6.0, ((0, 128),))
    return dict(tokens=tokens, gate_probs=gate_probs, expert_ids=expert_ids, placement=placement, replica=replica, row_counts=row_counts, w_gate=w_gate, w_up=w_up, w_down=w_down, d_out=d_out)


def silu_parts(gate_pre):
    sigma = jax.nn.sigmoid(gate_pre)
    return gate_pre * sigma, sigma * (1.0 + gate_pre * (1.0 - sigma))


def reference(tokens, gate_probs, expert_ids, placement, replica, row_counts, w_gate, w_up, w_down, d_out):
    pick_count = TOK_DEV * TOP_COUNT
    slot_count = DEVICES * CAP
    flat_ids = expert_ids.reshape(DEVICES, pick_count)
    flat_rep = replica.reshape(DEVICES, pick_count)
    dest_row = placement[flat_ids, flat_rep]
    target = dest_row * N_EXPERT + flat_ids
    token_pos = jnp.arange(pick_count, dtype=jnp.int32) // TOP_COUNT
    living = token_pos[None, :] < row_counts[:, None]
    dest_hits = (target[:, :, None] == jnp.arange(DEVICES, dtype=jnp.int32)[None, None, :]) & living[:, :, None]
    prefix_count = jnp.cumsum(dest_hits.astype(jnp.int32), axis=1) - 1
    rank_of = jnp.sum(jnp.where(dest_hits, prefix_count, 0), axis=2)
    keeping = living & (rank_of < CAP)
    source = jnp.arange(DEVICES, dtype=jnp.int32)[:, None]
    slot_place = target * slot_count + source * CAP + rank_of
    slot_place = jnp.where(keeping, slot_place, DEVICES * slot_count)
    global_pick = source * pick_count + jnp.arange(pick_count, dtype=jnp.int32)[None, :]
    slot_table = jnp.full((DEVICES * slot_count,), -1, jnp.int32)
    slot_table = slot_table.at[slot_place.reshape(-1)].set(global_pick.reshape(-1), mode="drop")
    slot_table = slot_table.reshape(N_DP, N_EXPERT, slot_count).transpose(1, 0, 2)
    gate_flat = gate_probs.reshape(-1)

    def per_expert(token_carry, expert_in):
        expert_slots, gate_mat, up_mat, down_mat = expert_in
        zero_grad = (jnp.zeros((D, F), jnp.float32), jnp.zeros((D, F), jnp.float32), jnp.zeros((F, D), jnp.float32))

        def per_row(row_carry, row_slots):
            (y_acc, dx_acc, dg_acc), (acc_g, acc_u, acc_d) = row_carry
            filled = row_slots >= 0
            safe_pick = jnp.where(filled, row_slots, 0)
            token_idx = safe_pick // TOP_COUNT
            weight = jnp.where(filled, gate_flat[safe_pick], 0.0)
            rows_x = jnp.where(filled[:, None], tokens[token_idx], 0)
            pre_g = jnp.dot(rows_x, gate_mat, preferred_element_type=jnp.float32)
            pre_u = jnp.dot(rows_x, up_mat, preferred_element_type=jnp.float32)
            silu_val, silu_slope = silu_parts(pre_g)
            hidden = (silu_val * pre_u).astype(jnp.bfloat16)
            expert_out = jnp.dot(hidden, down_mat, preferred_element_type=jnp.float32).astype(jnp.bfloat16)
            raw_cot = d_out[token_idx].astype(jnp.float32)
            cotan = (raw_cot * weight[:, None]).astype(jnp.bfloat16)
            d_hidden = jnp.dot(cotan, down_mat.T, preferred_element_type=jnp.float32)
            d_pre_g = (d_hidden * pre_u * silu_slope).astype(jnp.bfloat16)
            d_pre_u = (d_hidden * silu_val).astype(jnp.bfloat16)
            pick_dx = (jnp.dot(d_pre_g, gate_mat.T, preferred_element_type=jnp.float32)
                       + jnp.dot(d_pre_u, up_mat.T, preferred_element_type=jnp.float32)).astype(jnp.bfloat16)
            dims = (((0,), (0,)), ((), ()))
            part_g = lax.dot_general(rows_x, d_pre_g, dims, preferred_element_type=jnp.float32).astype(jnp.bfloat16)
            part_u = lax.dot_general(rows_x, d_pre_u, dims, preferred_element_type=jnp.float32).astype(jnp.bfloat16)
            part_d = lax.dot_general(hidden, cotan, dims, preferred_element_type=jnp.float32).astype(jnp.bfloat16)
            out_f = expert_out.astype(jnp.float32)
            y_acc = y_acc.at[token_idx].add(weight[:, None] * out_f)
            dx_acc = dx_acc.at[token_idx].add(jnp.where(filled[:, None], pick_dx.astype(jnp.float32), 0.0))
            dg_acc = dg_acc.at[safe_pick].add(jnp.where(filled, jnp.sum(raw_cot * out_f, axis=1), 0.0))
            grads = (acc_g + part_g.astype(jnp.float32), acc_u + part_u.astype(jnp.float32), acc_d + part_d.astype(jnp.float32))
            return ((y_acc, dx_acc, dg_acc), grads), None

        (token_carry, grads), _ = lax.scan(per_row, (token_carry, zero_grad), expert_slots)
        return token_carry, (grads[0].astype(jnp.bfloat16), grads[1].astype(jnp.bfloat16), grads[2].astype(jnp.bfloat16))

    start = (jnp.zeros((TOKENS, D), jnp.float32), jnp.zeros((TOKENS, D), jnp.float32),
             jnp.zeros((TOKENS * TOP_COUNT,), jnp.float32))
    (y_acc, dx_acc, dg_acc), (g_gate, g_up, g_down) = lax.scan(per_expert, start, (slot_table, w_gate, w_up, w_down))
    return (y_acc.astype(jnp.bfloat16), dx_acc.astype(jnp.bfloat16), dg_acc.reshape(TOKENS, TOP_COUNT),
            g_gate, g_up, g_down)
```

```python
import functools

import jax
import jax.numpy as jnp
from jax import lax
from jax.experimental import pallas as pl
from jax.experimental.pallas import tpu as pltpu
from jax.sharding import PartitionSpec as P

MESH = pl.DeviceIdType.MESH
BF = jnp.bfloat16
F32 = jnp.float32
CAP = 2


def dot_nn(a, b):
    return jnp.dot(a, b, preferred_element_type=F32)


def dot_nt(a, b):
    return lax.dot_general(a, b, (((1,), (1,)), ((), ())), preferred_element_type=F32)


def dot_tn(a, b):
    return lax.dot_general(a, b, (((0,), (0,)), ((), ())), preferred_element_type=F32)


def iota(shape, dim):
    return lax.broadcasted_iota(jnp.int32, shape, dim).astype(F32)


def moe_kernel(
    n_dp, n_e,
    count_ref, ids_c, ids_r, rep_c, rep_r, prob_c, prob_r, place_r, place_c,
    tokens, d_out, w_gate, w_up, w_down,
    layer_out, d_tokens, d_gates, g_gate, g_up, g_down,
    sel, pick0, pick1, wcol,
    wg, wu, wd,
    a_send, x_recv, b_send, c_recv, o_recv, d_recv,
    xs, cs, hs, gs, us,
    acc_g, acc_u, acc_h, own_part, part_send, part_recv,
    w_sem, yz_send, yz_recv, fw_send, fw_recv, ag_send, ag_recv, pt_send, pt_recv,
):
    nx = n_dp // 2
    rows = n_dp * CAP
    slots = rows * n_e
    toks, width = tokens.shape
    chunk = width // nx
    half = chunk // 2
    hid = acc_g.shape[1]
    p = lax.axis_index("dp")
    e = lax.axis_index("expert")
    x = p // 2
    core = p % 2

    def at_x(d):
        return {"dp": lax.rem(x + d, nx) * 2 + core}

    sibling = {"dp": x * 2 + 1 - core}

    def cols(j):
        return pl.ds(pl.multiple_of(lax.rem(x + 1 + j, nx) * chunk, chunk), chunk)

    barrier = pltpu.get_barrier_semaphore()

    def greet(d, _):
        pl.semaphore_signal(
            barrier, inc=1, device_id={"expert": lax.rem(e + d, n_e)}, device_id_type=MESH
        )
        return 0

    lax.fori_loop(1, n_e, greet, 0)
    for d in range(1, nx):
        pl.semaphore_signal(barrier, inc=1, device_id=at_x(d), device_id_type=MESH)
    pl.semaphore_signal(barrier, inc=1, device_id=sibling, device_id_type=MESH)

    def load_gate(j):
        return pltpu.make_async_copy(w_gate.at[0, cols(j)], wg.at[j], w_sem.at[0, j])

    def load_up(j):
        return pltpu.make_async_copy(w_up.at[0, cols(j)], wu.at[j], w_sem.at[1, j])

    def load_down(j):
        return pltpu.make_async_copy(w_down.at[0, :, cols(j)], wd.at[j], w_sem.at[2, j])

    for j in range(nx):
        load_gate(j).start()
        load_up(j).start()
    for j in range(nx):
        load_down(j).start()

    count = count_ref[0].astype(F32)
    codes = n_e * n_dp
    tgt_c, tgt_r, dst_c, dst_r, exp_c, exp_r = [], [], [], [], [], []
    for k in range(2):
        ec = ids_c[:, k : k + 1].astype(F32)
        er = ids_r[k : k + 1, :].astype(F32)
        code_c = ec * n_dp + rep_c[:, k : k + 1].astype(F32)
        code_r = er * n_dp + rep_r[k : k + 1, :].astype(F32)
        dc = jnp.sum(
            jnp.where(iota((toks, codes), 1) == code_c, place_r[...].astype(F32), 0.0),
            axis=1, keepdims=True,
        )
        dr = jnp.sum(
            jnp.where(iota((codes, toks), 0) == code_r, place_c[...].astype(F32), 0.0),
            axis=0, keepdims=True,
        )
        exp_c.append(ec)
        exp_r.append(er)
        dst_c.append(dc)
        dst_r.append(dr)
        tgt_c.append(dc * n_e + ec)
        tgt_r.append(dr * n_e + er)
    t_sub = iota((toks, toks), 0)
    t_lane = iota((toks, toks), 1)
    before_c = (t_lane < t_sub) & (t_lane < count)
    before_r = (t_sub < t_lane) & (t_sub < count)
    slot_c, slot_r = [], []
    for k in range(2):
        rank_c = jnp.zeros((toks, 1), F32)
        rank_r = jnp.zeros((1, toks), F32)
        for m in range(2):
            rank_c += jnp.sum(
                jnp.where((tgt_c[k] == tgt_r[m]) & before_c, 1.0, 0.0), axis=1, keepdims=True
            )
            rank_r += jnp.sum(
                jnp.where((tgt_c[m] == tgt_r[k]) & before_r, 1.0, 0.0), axis=0, keepdims=True
            )
        keep_c = (rank_c < CAP) & (iota((toks, 1), 0) < count)
        keep_r = (rank_r < CAP) & (iota((1, toks), 1) < count)
        slot_c.append(jnp.where(keep_c, exp_c[k] * rows + dst_c[k] * CAP + rank_c, -1.0))
        slot_r.append(jnp.where(keep_r, exp_r[k] * rows + dst_r[k] * CAP + rank_r, -1.0))
    slot_sub = iota((slots, toks), 0)
    slot_lane = iota((toks, slots), 1)
    hit0 = slot_sub == slot_r[0]
    hit1 = slot_sub == slot_r[1]
    sel[...] = jnp.where(hit0 | hit1, 1.0, 0.0).astype(BF)
    wcol[...] = jnp.sum(
        jnp.where(hit0, prob_r[0:1, :], 0.0) + jnp.where(hit1, prob_r[1:2, :], 0.0),
        axis=1, keepdims=True,
    )
    pick0[...] = jnp.where(slot_lane == slot_c[0], 1.0, 0.0).astype(BF)
    pick1[...] = jnp.where(slot_lane == slot_c[1], 1.0, 0.0).astype(BF)

    def block(i):
        return pl.ds(pl.multiple_of(i * rows, rows), rows)

    def exchange(stage, src, dst, j):
        def one(d, _):
            q = lax.rem(e + d, n_e)
            pltpu.make_async_remote_copy(
                src.at[j, block(q)], dst.at[j, block(e)],
                yz_send.at[stage, j], yz_recv.at[stage, j],
                device_id={"expert": q}, device_id_type=MESH,
            ).start()
            return 0

        lax.fori_loop(1, n_e, one, 0)
        pltpu.make_async_copy(
            src.at[j, block(e)], dst.at[j, block(e)], yz_recv.at[stage, j]
        ).start()

    def arrived(stage, dst, j):
        pltpu.make_async_copy(dst.at[j], dst.at[j], yz_recv.at[stage, j]).wait()

    def sent(stage, src, j):
        part = src.at[j, pl.ds(0, slots - rows)]
        pltpu.make_async_copy(part, part, yz_send.at[stage, j]).wait()

    def forward(which, src, dst, j):
        return pltpu.make_async_remote_copy(
            src.at[j], dst.at[j], fw_send.at[which, j], fw_recv.at[which, j],
            device_id=at_x(j + 1), device_id_type=MESH,
        )

    def spread(which, buf, d):
        return pltpu.make_async_remote_copy(
            buf.at[0], buf.at[d], ag_send.at[which, d - 1], ag_recv.at[which, d - 1],
            device_id=at_x(d), device_id_type=MESH,
        )

    def gather_x(j):
        a_send[j] = dot_nn(sel[...], tokens[:, cols(j)]).astype(BF)

    gather_x(0)
    pl.semaphore_wait(barrier, n_e - 1 + nx - 1 + 1)
    exchange(0, a_send, x_recv, 0)

    def first(j, _):
        gather_x(j)
        exchange(0, a_send, x_recv, j)
        return 0

    lax.fori_loop(1, nx, first, 0)

    def gather_cot(j, _):
        raw = dot_nn(sel[...], d_out[:, cols(j)])
        b_send[j] = (raw * wcol[...]).astype(BF)
        return 0

    lax.fori_loop(0, nx, gather_cot, 0)

    acc_g[...] = jnp.zeros_like(acc_g)
    acc_u[...] = jnp.zeros_like(acc_u)
    acc_h[...] = jnp.zeros_like(acc_h)

    def pre_step(j, _):
        arrived(0, x_recv, j)
        exchange(1, b_send, c_recv, j)

        @pl.when(j < nx - 1)
        def _():
            forward(0, x_recv, xs, j).start()

        load_gate(j).wait()
        load_up(j).wait()
        acc_g[...] += dot_nn(x_recv[j], wg[j])
        acc_u[...] += dot_nn(x_recv[j], wu[j])
        return 0

    lax.fori_loop(0, nx, pre_step, 0)

    band = min(32, slots)

    def activate(i, _):
        r = pl.ds(pl.multiple_of(i * band, band), band)
        pre_g = acc_g[r, :]
        pre_u = acc_u[r, :]
        sig = jax.nn.sigmoid(pre_g)
        val = pre_g * sig
        hs[0, r, :] = (val * pre_u).astype(BF)
        acc_g[r, :] = pre_u * (sig * (1.0 + pre_g * (1.0 - sig)))
        acc_u[r, :] = val
        return 0

    lax.fori_loop(0, slots // band, activate, 0)
    for d in range(1, nx):
        spread(0, hs, d).start()

    def cot_step(j, _):
        arrived(1, c_recv, j)

        @pl.when(j < nx - 1)
        def _():
            forward(1, c_recv, cs, j).start()

        load_down(j).wait()
        sent(0, a_send, j)
        a_send[j] = dot_nn(hs[0], wd[j]).astype(BF)
        exchange(2, a_send, o_recv, j)
        acc_h[...] += dot_nt(c_recv[j], wd[j])
        return 0

    lax.fori_loop(0, nx, cot_step, 0)

    def slopes(i, _):
        r = pl.ds(pl.multiple_of(i * band, band), band)
        d_h = acc_h[r, :]
        gs[0, r, :] = (d_h * acc_g[r, :]).astype(BF)
        us[0, r, :] = (d_h * acc_u[r, :]).astype(BF)
        return 0

    lax.fori_loop(0, slots // band, slopes, 0)
    for d in range(1, nx):
        spread(1, gs, d).start()
    for d in range(1, nx):
        spread(2, us, d).start()

    def dx_step(j, _):
        sent(1, b_send, j)
        b_send[j] = (dot_nt(gs[0], wg[j]) + dot_nt(us[0], wu[j])).astype(BF)
        exchange(3, b_send, d_recv, j)
        return 0

    lax.fori_loop(0, nx, dx_step, 0)

    def out_step(j, carry):
        g0, g1 = carry
        arrived(2, o_recv, j)
        got = o_recv[j]
        out0 = dot_nn(pick0[...], got)
        out1 = dot_nn(pick1[...], got)
        cot = d_out[:, cols(j)].astype(F32)
        layer_out[:, cols(j)] = (prob_c[:, 0:1] * out0 + prob_c[:, 1:2] * out1).astype(BF)
        g0 = g0 + jnp.sum(cot * out0, axis=1, keepdims=True)
        g1 = g1 + jnp.sum(cot * out1, axis=1, keepdims=True)
        return g0, g1

    zero = jnp.zeros((toks, 1), F32)
    g0, g1 = lax.fori_loop(0, nx, out_step, (zero, zero))
    d_gates[...] = jnp.where(lax.broadcasted_iota(jnp.int32, (toks, 2), 1) == 0, g0, g1)

    tile = half // 2 if half % 256 == 0 else half

    def row_block(which, d):
        if which == 0:
            return x_recv.at[nx - 1] if d == 0 else xs.at[d - 1]
        return c_recv.at[nx - 1] if d == 0 else cs.at[d - 1]

    def grad_tile(which, start):
        c = pl.ds(pl.multiple_of(start, tile), tile)
        total = None
        for d in range(nx):
            if which == 2:
                term = dot_tn(hs[d], row_block(1, d)[:, c])
            else:
                term = dot_tn(row_block(0, d)[:, c], (gs if which == 0 else us)[d])
            total = term if total is None else total + term
        return total

    def part_copy(which):
        return pltpu.make_async_remote_copy(
            part_send.at[which], part_recv.at[which], pt_send.at[which], pt_recv.at[which],
            device_id=sibling, device_id_type=MESH,
        )

    def put(ref, which, t, value):
        if which == 2:
            ref[t] = value
        else:
            ref[which, pl.ds(t * tile, tile), :] = value

    def grads(which):
        for d in range(1, nx):
            if which == 2:
                forward(1, c_recv, cs, d - 1).wait_recv()
                spread(0, hs, d).wait_recv()
            elif which == 0:
                forward(0, x_recv, xs, d - 1).wait_recv()
                spread(1, gs, d).wait_recv()
            else:
                spread(2, us, d).wait_recv()

    down_send, down_own, down_recv = part_send[1], own_part[1], part_recv[1]
    part_send, own_part, part_recv = part_send[0], own_part[0], part_recv[0]

    def down_copy():
        return pltpu.make_async_remote_copy(
            down_send, down_recv, pt_send.at[2], pt_recv.at[2],
            device_id=sibling, device_id_type=MESH,
        )

    grads(2)
    for t in range(half // tile):
        down_send[:, pl.ds(t * tile, tile)] = grad_tile(2, (1 - core) * half + t * tile).astype(BF)
    down_copy().start()
    for t in range(half // tile):
        down_own[:, pl.ds(t * tile, tile)] = grad_tile(2, core * half + t * tile)
    for which in (0, 1):
        grads(which)
        for t in range(half // tile):
            part_send[which, pl.ds(t * tile, tile), :] = grad_tile(
                which, (1 - core) * half + t * tile
            ).astype(BF)
        part_copy(which).start()
        for t in range(half // tile):
            own_part[which, pl.ds(t * tile, tile), :] = grad_tile(which, core * half + t * tile)

    def tok_step(j, _):
        arrived(3, d_recv, j)
        both = pick0[...] + pick1[...]
        d_tokens[:, cols(j)] = dot_nn(both, d_recv[j]).astype(BF)
        return 0

    lax.fori_loop(0, nx, tok_step, 0)

    down_copy().wait_recv()
    g_down[0] = (down_own[...] + down_recv[...].astype(F32)).astype(BF)
    part_copy(0).wait_recv()
    g_gate[0] = (own_part[0] + part_recv[0].astype(F32)).astype(BF)
    part_copy(1).wait_recv()
    g_up[0] = (own_part[1] + part_recv[1].astype(F32)).astype(BF)

    down_copy().wait_send()
    for which in (0, 1):
        part_copy(which).wait_send()

    def drain(j, _):
        sent(2, a_send, j)
        sent(3, b_send, j)
        return 0

    lax.fori_loop(0, nx, drain, 0)
    for d in range(1, nx):
        forward(0, x_recv, xs, d - 1).wait_send()
        forward(1, c_recv, cs, d - 1).wait_send()
        spread(0, hs, d).wait_send()
        spread(1, gs, d).wait_send()
        spread(2, us, d).wait_send()


def on_device(
    tokens, gate_probs, expert_ids, placement, replica, row_counts, w_gate, w_up, w_down, d_out
):
    n_dp = lax.axis_size("dp")
    n_e = lax.axis_size("expert")
    nx = n_dp // 2
    toks, width = tokens.shape
    hid = w_gate.shape[2]
    slots = n_dp * CAP * n_e
    chunk = width // nx
    half = chunk // 2
    vmem = pl.BlockSpec(memory_space=pltpu.VMEM)
    hbm = pl.BlockSpec(memory_space=pl.ANY)
    smem = pl.BlockSpec(memory_space=pltpu.SMEM)
    yz = (nx, slots, chunk)
    near = (nx - 1, slots, chunk)
    wide = (nx, slots, hid)
    dma = pltpu.SemaphoreType.DMA
    flops = 18 * slots * width * hid
    return pl.pallas_call(
        functools.partial(moe_kernel_entry, n_dp, n_e),
        out_shape=(
            jax.ShapeDtypeStruct((toks, width), BF),
            jax.ShapeDtypeStruct((toks, width), BF),
            jax.ShapeDtypeStruct((toks, 2), F32),
            jax.ShapeDtypeStruct((1, half, hid), BF),
            jax.ShapeDtypeStruct((1, half, hid), BF),
            jax.ShapeDtypeStruct((1, hid, half), BF),
        ),
        in_specs=[smem] + [vmem] * 10 + [hbm] * 3,
        out_specs=[vmem] * 6,
        scratch_shapes=[
            pltpu.VMEM((slots, toks), BF),
            pltpu.VMEM((toks, slots), BF),
            pltpu.VMEM((toks, slots), BF),
            pltpu.VMEM((slots, 1), F32),
            pltpu.VMEM((nx, chunk, hid), BF),
            pltpu.VMEM((nx, chunk, hid), BF),
            pltpu.VMEM((nx, hid, chunk), BF),
            pltpu.VMEM(yz, BF),
            pltpu.VMEM(yz, BF),
            pltpu.VMEM(yz, BF),
            pltpu.VMEM(yz, BF),
            pltpu.VMEM(yz, BF),
            pltpu.VMEM(yz, BF),
            pltpu.VMEM(near, BF),
            pltpu.VMEM(near, BF),
            pltpu.VMEM(wide, BF),
            pltpu.VMEM(wide, BF),
            pltpu.VMEM(wide, BF),
            pltpu.VMEM((slots, hid), F32),
            pltpu.VMEM((slots, hid), F32),
            pltpu.VMEM((slots, hid), F32),
            pltpu.VMEM((2, half, hid), F32),
            pltpu.VMEM((hid, half), F32),
            pltpu.VMEM((2, half, hid), BF),
            pltpu.VMEM((hid, half), BF),
            pltpu.VMEM((2, half, hid), BF),
            pltpu.VMEM((hid, half), BF),
            dma((3, nx)),
            dma((4, nx)),
            dma((4, nx)),
            dma((2, nx - 1)),
            dma((2, nx - 1)),
            dma((3, nx - 1)),
            dma((3, nx - 1)),
            dma((3,)),
            dma((3,)),
        ],
        compiler_params=pltpu.CompilerParams(
            collective_id=0, has_side_effects=True, vmem_limit_bytes=62 << 20
        ),
        cost_estimate=pl.CostEstimate(flops=flops, bytes_accessed=6 * width * hid, transcendentals=0),
        name="moe",
    )(
        row_counts, expert_ids, expert_ids.T, replica, replica.T, gate_probs, gate_probs.T,
        placement.reshape(1, n_e * n_dp), placement.reshape(n_e * n_dp, 1),
        tokens, d_out, w_gate, w_up, w_down,
    )


def moe_kernel_entry(n_dp, n_e, *refs):
    head, rest = refs[:41], refs[41:]
    own_part, down_own, part_send, down_send, part_recv, down_recv = rest[:6]
    moe_kernel(
        n_dp, n_e, *head,
        (own_part, down_own), (part_send, down_send), (part_recv, down_recv), *rest[6:],
    )


def solution(mesh):
    rows = P(("dp", "expert"), None)
    weight = P("expert", None, None)
    return jax.shard_map(
        on_device,
        mesh=mesh,
        in_specs=(
            rows, rows, rows, P(), rows, P(("dp", "expert")), weight, weight, weight, rows,
        ),
        out_specs=(
            rows, rows, rows,
            P("expert", "dp", None), P("expert", "dp", None), P("expert", None, "dp"),
        ),
        check_vma=False,
    )
```

```python
import functools

import jax
import jax.numpy as jnp
from jax import lax
from jax.experimental import pallas as pl
from jax.experimental.pallas import tpu as pltpu
from jax.sharding import PartitionSpec as P

MESH = pl.DeviceIdType.MESH
BF = jnp.bfloat16
F32 = jnp.float32
CAP = 2


def dot_nn(a, b):
    return jnp.dot(a, b, preferred_element_type=F32)


def dot_nt(a, b):
    return lax.dot_general(a, b, (((1,), (1,)), ((), ())), preferred_element_type=F32)


def dot_tn(a, b):
    return lax.dot_general(a, b, (((0,), (0,)), ((), ())), preferred_element_type=F32)


def iota(shape, dim):
    return lax.broadcasted_iota(jnp.int32, shape, dim).astype(F32)


def moe_kernel(
    n_dp, n_e,
    count_ref, ids_r, rep_r, prob_r, place_t,
    tokens_hbm, d_out_hbm, w_gate, w_up, w_down,
    layer_out, d_tokens, d_gates, g_gate, g_up, g_down,
    tokens, d_out, lo_buf, dt_buf,
    sel, pick0, pick1, wcol, prob_c,
    wg, wu, wd,
    a_send, x_recv, b_send, c_recv, o_recv, d_recv,
    xs, cs, hs, gs, us,
    acc_g, acc_u, acc_h,
    gu_own, down_own, gu_send, down_send, gu_recv, down_recv, gu_out, down_out,
    w_sem, t_sem, out_sem,
    yz_send, yz_recv, fw_send, fw_recv, ag_send, ag_recv, pt_send, pt_recv,
):
    nx = n_dp // 2
    rows = n_dp * CAP
    slots = rows * n_e
    toks, width = tokens_hbm.shape
    chunk = width // nx
    half = chunk // 2
    p = lax.axis_index("dp")
    e = lax.axis_index("expert")
    x = p // 2
    core = p % 2

    def at_x(d):
        return {"dp": lax.rem(x + d, nx) * 2 + core}

    sibling = {"dp": x * 2 + 1 - core}

    def cols(j):
        return pl.ds(pl.multiple_of(lax.rem(x + 1 + j, nx) * chunk, chunk), chunk)

    barrier = pltpu.get_barrier_semaphore()

    def greet(d, _):
        pl.semaphore_signal(
            barrier, inc=1, device_id={"expert": lax.rem(e + d, n_e)}, device_id_type=MESH
        )
        return 0

    lax.fori_loop(1, n_e, greet, 0)
    for d in range(1, nx):
        pl.semaphore_signal(barrier, inc=1, device_id=at_x(d), device_id_type=MESH)
    pl.semaphore_signal(barrier, inc=1, device_id=sibling, device_id_type=MESH)

    def load_gate(j):
        return pltpu.make_async_copy(w_gate.at[0, cols(j)], wg.at[j], w_sem.at[0, j])

    def load_up(j):
        return pltpu.make_async_copy(w_up.at[0, cols(j)], wu.at[j], w_sem.at[1, j])

    def load_down(j):
        return pltpu.make_async_copy(w_down.at[0, :, cols(j)], wd.at[j], w_sem.at[2, j])

    def load_tok(j):
        return pltpu.make_async_copy(tokens_hbm.at[:, cols(j)], tokens.at[j], t_sem.at[0, j])

    def load_cot(j):
        return pltpu.make_async_copy(d_out_hbm.at[:, cols(j)], d_out.at[j], t_sem.at[1, j])

    for j in range(nx):
        load_tok(j).start()
    for j in range(nx):
        load_cot(j).start()
        load_gate(j).start()
        load_up(j).start()
    for j in range(nx):
        load_down(j).start()

    count = count_ref[0].astype(F32)
    place = place_t[...].astype(F32).astype(BF)
    tgt_r, dst_r, exp_r = [], [], []
    for k in range(2):
        er = ids_r[k : k + 1, :].astype(F32)
        rr = rep_r[k : k + 1, :].astype(F32)
        of_expert = jnp.where(iota((n_e, toks), 0) == er, 1.0, 0.0).astype(BF)
        holders = dot_nn(place, of_expert)
        dr = jnp.sum(jnp.where(iota((n_dp, toks), 0) == rr, holders, 0.0), axis=0, keepdims=True)
        exp_r.append(er)
        dst_r.append(dr)
        tgt_r.append(dr * n_e + er)
    t_sub = iota((toks, toks), 0)
    t_lane = iota((toks, toks), 1)
    diagonal = t_sub == t_lane

    def as_column(row):
        return jnp.sum(jnp.where(diagonal, row, 0.0), axis=1, keepdims=True)

    tgt_c = [as_column(tgt_r[k]) for k in range(2)]
    before = (t_sub < t_lane) & (t_sub < count)
    slot_r = []
    for k in range(2):
        rank = jnp.zeros((1, toks), F32)
        for m in range(2):
            rank += jnp.sum(
                jnp.where((tgt_c[m] == tgt_r[k]) & before, 1.0, 0.0), axis=0, keepdims=True
            )
        keep = (rank < CAP) & (iota((1, toks), 1) < count)
        slot_r.append(jnp.where(keep, exp_r[k] * rows + dst_r[k] * CAP + rank, -1.0))
    slot_sub = iota((slots, toks), 0)
    slot_lane = iota((toks, slots), 1)
    hit0 = slot_sub == slot_r[0]
    hit1 = slot_sub == slot_r[1]
    sel[...] = jnp.where(hit0 | hit1, 1.0, 0.0).astype(BF)
    wcol[...] = jnp.sum(
        jnp.where(hit0, prob_r[0:1, :], 0.0) + jnp.where(hit1, prob_r[1:2, :], 0.0),
        axis=1, keepdims=True,
    )

    def rest_of_routing():
        pick0[...] = jnp.where(slot_lane == as_column(slot_r[0]), 1.0, 0.0).astype(BF)
        pick1[...] = jnp.where(slot_lane == as_column(slot_r[1]), 1.0, 0.0).astype(BF)
        prob_c[0] = as_column(prob_r[0:1, :])
        prob_c[1] = as_column(prob_r[1:2, :])

    def block(i):
        return pl.ds(pl.multiple_of(i * rows, rows), rows)

    def exchange(stage, src, dst, j):
        def one(d, _):
            q = lax.rem(e + d, n_e)
            pltpu.make_async_remote_copy(
                src.at[j, block(q)], dst.at[j, block(e)],
                yz_send.at[stage, j], yz_recv.at[stage, j],
                device_id={"expert": q}, device_id_type=MESH,
            ).start()
            return 0

        lax.fori_loop(1, n_e, one, 0)
        pltpu.make_async_copy(
            src.at[j, block(e)], dst.at[j, block(e)], yz_recv.at[stage, j]
        ).start()

    def arrived(stage, dst, j):
        pltpu.make_async_copy(dst.at[j], dst.at[j], yz_recv.at[stage, j]).wait()

    def sent(stage, src, j):
        part = src.at[j, pl.ds(0, slots - rows)]
        pltpu.make_async_copy(part, part, yz_send.at[stage, j]).wait()

    def forward(which, src, dst, j):
        return pltpu.make_async_remote_copy(
            src.at[j], dst.at[j], fw_send.at[which, j], fw_recv.at[which, j],
            device_id=at_x(j + 1), device_id_type=MESH,
        )

    cut = slots // 2

    def hand(which, buf, way):
        return pltpu.make_async_remote_copy(
            buf.at[0], buf.at[1 if way == 0 else nx - 1],
            ag_send.at[which, way], ag_recv.at[which, way],
            device_id=at_x(1 if way == 0 else nx - 1), device_id_type=MESH,
        )

    def relay(which, buf, way):
        r = pl.ds(way * cut, cut)
        return pltpu.make_async_remote_copy(
            buf.at[1 if way == 0 else nx - 1, r], buf.at[2, r],
            ag_send.at[which, 2 + way], ag_recv.at[which, 2 + way],
            device_id=at_x(1 if way == 0 else nx - 1), device_id_type=MESH,
        )

    def hand_out(which, buf):
        for way in (0, 1):
            hand(which, buf, way).start()

    def pass_on(which, buf):
        for way in (0, 1):
            hand(which, buf, way).wait_recv()
            relay(which, buf, way).start()

    def all_here(which, buf):
        for way in (0, 1):
            relay(which, buf, way).wait_recv()

    def gather_x(j):
        load_tok(j).wait()
        a_send[j] = dot_nn(sel[...], tokens[j]).astype(BF)

    gather_x(0)
    pl.semaphore_wait(barrier, n_e - 1 + nx - 1 + 1)
    exchange(0, a_send, x_recv, 0)

    def first(j, _):
        gather_x(j)
        exchange(0, a_send, x_recv, j)
        return 0

    lax.fori_loop(1, nx, first, 0)
    rest_of_routing()

    def gather_cot(j, _):
        load_cot(j).wait()
        raw = dot_nn(sel[...], d_out[j])
        b_send[j] = (raw * wcol[...]).astype(BF)
        return 0

    lax.fori_loop(0, nx, gather_cot, 0)

    acc_g[...] = jnp.zeros_like(acc_g)
    acc_u[...] = jnp.zeros_like(acc_u)
    acc_h[...] = jnp.zeros_like(acc_h)

    def pre_step(j, _):
        arrived(0, x_recv, j)
        exchange(1, b_send, c_recv, j)

        @pl.when(j < nx - 1)
        def _():
            forward(0, x_recv, xs, j).start()

        load_gate(j).wait()
        load_up(j).wait()
        acc_g[...] += dot_nn(x_recv[j], wg[j])
        acc_u[...] += dot_nn(x_recv[j], wu[j])
        return 0

    lax.fori_loop(0, nx, pre_step, 0)

    band = min(32, slots)

    def activate(i, _):
        r = pl.ds(pl.multiple_of(i * band, band), band)
        pre_g = acc_g[r, :]
        pre_u = acc_u[r, :]
        sig = jax.nn.sigmoid(pre_g)
        val = pre_g * sig
        hs[0, r, :] = (val * pre_u).astype(BF)
        acc_g[r, :] = pre_u * (sig * (1.0 + pre_g * (1.0 - sig)))
        acc_u[r, :] = val
        return 0

    lax.fori_loop(0, slots // band, activate, 0)
    hand_out(0, hs)

    def cot_step(j, _):
        @pl.when(j == nx - 1)
        def _():
            pass_on(0, hs)

        arrived(1, c_recv, j)

        @pl.when(j < nx - 1)
        def _():
            forward(1, c_recv, cs, j).start()

        load_down(j).wait()
        sent(0, a_send, j)
        a_send[j] = dot_nn(hs[0], wd[j]).astype(BF)
        exchange(2, a_send, o_recv, j)
        acc_h[...] += dot_nt(c_recv[j], wd[j])
        return 0

    lax.fori_loop(0, nx, cot_step, 0)

    def slopes(i, _):
        r = pl.ds(pl.multiple_of(i * band, band), band)
        d_h = acc_h[r, :]
        gs[0, r, :] = (d_h * acc_g[r, :]).astype(BF)
        us[0, r, :] = (d_h * acc_u[r, :]).astype(BF)
        return 0

    lax.fori_loop(0, slots // band, slopes, 0)
    hand_out(1, gs)
    hand_out(2, us)

    def dx_step(j, _):
        sent(1, b_send, j)
        b_send[j] = (dot_nt(gs[0], wg[j]) + dot_nt(us[0], wu[j])).astype(BF)
        exchange(3, b_send, d_recv, j)
        return 0

    lax.fori_loop(0, nx, dx_step, 0)

    def out_copy(j):
        return pltpu.make_async_copy(lo_buf.at[j], layer_out.at[:, cols(j)], out_sem.at[0, j])

    def tok_copy(j):
        return pltpu.make_async_copy(dt_buf.at[j], d_tokens.at[:, cols(j)], out_sem.at[1, j])

    def out_step(j, carry):
        g0, g1 = carry

        @pl.when(j == nx - 2)
        def _():
            pass_on(1, gs)

        @pl.when(j == nx - 1)
        def _():
            pass_on(2, us)

        arrived(2, o_recv, j)
        got = o_recv[j]
        out0 = dot_nn(pick0[...], got)
        out1 = dot_nn(pick1[...], got)
        cot = d_out[j].astype(F32)
        lo_buf[j] = (prob_c[0] * out0 + prob_c[1] * out1).astype(BF)
        out_copy(j).start()
        g0 = g0 + jnp.sum(cot * out0, axis=1, keepdims=True)
        g1 = g1 + jnp.sum(cot * out1, axis=1, keepdims=True)
        return g0, g1

    zero = jnp.zeros((toks, 1), F32)
    g0, g1 = lax.fori_loop(0, nx, out_step, (zero, zero))

    def as_row(column):
        return jnp.sum(jnp.where(diagonal, column, 0.0), axis=0, keepdims=True)

    d_gates[0:1, :] = as_row(g0)
    d_gates[1:2, :] = as_row(g1)

    tile = half // 2 if half % 256 == 0 else half

    def row_block(which, d):
        if which == 0:
            return x_recv.at[nx - 1] if d == 0 else xs.at[d - 1]
        return c_recv.at[nx - 1] if d == 0 else cs.at[d - 1]

    def grad_tile(which, start):
        c = pl.ds(pl.multiple_of(start, tile), tile)
        total = None
        for d in range(nx):
            if which == 2:
                term = dot_tn(hs[d], row_block(1, d)[:, c])
            else:
                term = dot_tn(row_block(0, d)[:, c], (gs if which == 0 else us)[d])
            total = term if total is None else total + term
        return total

    def part_copy(which):
        src, dst = (gu_send.at[which], gu_recv.at[which]) if which < 2 else (down_send, down_recv)
        return pltpu.make_async_remote_copy(
            src, dst, pt_send.at[which], pt_recv.at[which],
            device_id=sibling, device_id_type=MESH,
        )

    def grad_copy(which):
        if which == 2:
            return pltpu.make_async_copy(down_out, g_down.at[0], out_sem.at[2, 2])
        return pltpu.make_async_copy(
            gu_out.at[which], (g_gate, g_up)[which].at[0], out_sem.at[2, which]
        )

    def grads(which):
        if which == 2:
            for d in range(1, nx):
                forward(1, c_recv, cs, d - 1).wait_recv()
            all_here(0, hs)
        elif which == 0:
            for d in range(1, nx):
                forward(0, x_recv, xs, d - 1).wait_recv()
            all_here(1, gs)
        else:
            all_here(2, us)
        for t in range(half // tile):
            value = grad_tile(which, (1 - core) * half + t * tile).astype(BF)
            if which == 2:
                down_send[:, pl.ds(t * tile, tile)] = value
            else:
                gu_send[which, pl.ds(t * tile, tile), :] = value
        part_copy(which).start()
        for t in range(half // tile):
            value = grad_tile(which, core * half + t * tile)
            if which == 2:
                down_own[:, pl.ds(t * tile, tile)] = value
            else:
                gu_own[which, pl.ds(t * tile, tile), :] = value

    def finish(which):
        part_copy(which).wait_recv()
        if which == 2:
            down_out[...] = (down_own[...] + down_recv[...].astype(F32)).astype(BF)
        else:
            gu_out[which] = (gu_own[which] + gu_recv[which].astype(F32)).astype(BF)
        grad_copy(which).start()

    def tok_step(j):
        arrived(3, d_recv, j)
        dt_buf[j] = dot_nn(pick0[...] + pick1[...], d_recv[j]).astype(BF)
        tok_copy(j).start()

    grads(2)
    finish(2)
    tok_step(0)
    grads(0)
    tok_step(1)
    grads(1)
    finish(0)
    tok_step(2)
    finish(1)
    tok_step(3)

    for which in range(3):
        part_copy(which).wait_send()
        grad_copy(which).wait()

    def drain(j, _):
        sent(2, a_send, j)
        sent(3, b_send, j)
        out_copy(j).wait()
        tok_copy(j).wait()
        return 0

    lax.fori_loop(0, nx, drain, 0)
    for d in range(1, nx):
        forward(0, x_recv, xs, d - 1).wait_send()
        forward(1, c_recv, cs, d - 1).wait_send()
    for which, buf in enumerate((hs, gs, us)):
        for way in (0, 1):
            hand(which, buf, way).wait_send()
            relay(which, buf, way).wait_send()


def place_kernel(*refs):
    n = (len(refs) - 1) // 3
    src, dst, hold, sems = refs[:n], refs[n : 2 * n], refs[2 * n : 3 * n], refs[-1]
    loads, stores = [], []
    for i in range(n):
        dim = len(src[i].shape) - 2
        pieces = 2 if src[i].shape[dim] >= 32 else 1
        size = src[i].shape[dim] // pieces
        for piece in range(pieces):
            at = (slice(None),) * dim + (pl.ds(piece * size, size),)
            loads.append(pltpu.make_async_copy(src[i].at[at], hold[i].at[at], sems.at[0, i, piece]))
            stores.append(pltpu.make_async_copy(hold[i].at[at], dst[i].at[at], sems.at[1, i, piece]))
    for copy in loads:
        copy.start()
    for load, store in zip(loads, stores):
        load.wait()
        store.start()
    for copy in stores:
        copy.wait()


def on_device(
    tokens, gate_probs, expert_ids, placement, replica, row_counts, w_gate, w_up, w_down, d_out
):
    n_dp = lax.axis_size("dp")
    n_e = lax.axis_size("expert")
    nx = n_dp // 2
    toks, width = tokens.shape
    hid = w_gate.shape[2]
    slots = n_dp * CAP * n_e
    chunk = width // nx
    half = chunk // 2
    vmem = pl.BlockSpec(memory_space=pltpu.VMEM)
    hbm = pl.BlockSpec(memory_space=pl.ANY)
    smem = pl.BlockSpec(memory_space=pltpu.SMEM)
    yz = (nx, slots, chunk)
    near = (nx - 1, slots, chunk)
    wide = (nx, slots, hid)
    dma = pltpu.SemaphoreType.DMA
    flops = 18 * slots * width * hid
    outs = (
        jax.ShapeDtypeStruct((toks, width), BF),
        jax.ShapeDtypeStruct((toks, width), BF),
        jax.ShapeDtypeStruct((2, toks), F32),
        jax.ShapeDtypeStruct((1, half, hid), BF),
        jax.ShapeDtypeStruct((1, half, hid), BF),
        jax.ShapeDtypeStruct((1, hid, half), BF),
    )
    mine = (nx, toks, chunk)
    results = pl.pallas_call(
        functools.partial(moe_kernel, n_dp, n_e),
        out_shape=outs,
        in_specs=[smem] + [vmem] * 4 + [hbm] * 5,
        out_specs=[hbm, hbm, vmem, hbm, hbm, hbm],
        scratch_shapes=[
            pltpu.VMEM(mine, BF),
            pltpu.VMEM(mine, BF),
            pltpu.VMEM(mine, BF),
            pltpu.VMEM(mine, BF),
            pltpu.VMEM((slots, toks), BF),
            pltpu.VMEM((toks, slots), BF),
            pltpu.VMEM((toks, slots), BF),
            pltpu.VMEM((slots, 1), F32),
            pltpu.VMEM((2, toks, 1), F32),
            pltpu.VMEM((nx, chunk, hid), BF),
            pltpu.VMEM((nx, chunk, hid), BF),
            pltpu.VMEM((nx, hid, chunk), BF),
            pltpu.VMEM(yz, BF),
            pltpu.VMEM(yz, BF),
            pltpu.VMEM(yz, BF),
            pltpu.VMEM(yz, BF),
            pltpu.VMEM(yz, BF),
            pltpu.VMEM(yz, BF),
            pltpu.VMEM(near, BF),
            pltpu.VMEM(near, BF),
            pltpu.VMEM(wide, BF),
            pltpu.VMEM(wide, BF),
            pltpu.VMEM(wide, BF),
            pltpu.VMEM((slots, hid), F32),
            pltpu.VMEM((slots, hid), F32),
            pltpu.VMEM((slots, hid), F32),
            pltpu.VMEM((2, half, hid), F32),
            pltpu.VMEM((hid, half), F32),
            pltpu.VMEM((2, half, hid), BF),
            pltpu.VMEM((hid, half), BF),
            pltpu.VMEM((2, half, hid), BF),
            pltpu.VMEM((hid, half), BF),
            pltpu.VMEM((2, half, hid), BF),
            pltpu.VMEM((hid, half), BF),
            dma((3, nx)),
            dma((2, nx)),
            dma((3, nx)),
            dma((4, nx)),
            dma((4, nx)),
            dma((2, nx - 1)),
            dma((2, nx - 1)),
            dma((3, 4)),
            dma((3, 4)),
            dma((3,)),
            dma((3,)),
        ],
        compiler_params=pltpu.CompilerParams(
            collective_id=0, has_side_effects=True, vmem_limit_bytes=62 << 20
        ),
        cost_estimate=pl.CostEstimate(flops=flops, bytes_accessed=6 * width * hid, transcendentals=0),
        name="moe",
    )(
        row_counts, expert_ids.T, replica.T, gate_probs.T, placement.T,
        tokens, d_out, w_gate, w_up, w_down,
    )
    results = pl.pallas_call(
        place_kernel,
        out_shape=outs,
        in_specs=[hbm] * 6,
        out_specs=[hbm] * 6,
        scratch_shapes=[pltpu.VMEM(out.shape, out.dtype) for out in outs] + [dma((2, 6, 2))],
        name="place",
    )(*results)
    layer_out, d_tokens, d_gates, g_gate, g_up, g_down = results
    return layer_out, d_tokens, d_gates.T, g_gate, g_up, g_down


def solution(mesh):
    rows = P(("dp", "expert"), None)
    weight = P("expert", None, None)
    return jax.shard_map(
        on_device,
        mesh=mesh,
        in_specs=(
            rows, rows, rows, P(), rows, P(("dp", "expert")), weight, weight, weight, rows,
        ),
        out_specs=(
            rows, rows, rows,
            P("expert", "dp", None), P("expert", "dp", None), P("expert", None, "dp"),
        ),
        check_vma=False,
    )
```

```python
import functools

import jax
import jax.numpy as jnp
from jax import lax
from jax.experimental import pallas as pl
from jax.experimental.pallas import tpu as pltpu
from jax.sharding import PartitionSpec as P

MESH = pl.DeviceIdType.MESH
BF = jnp.bfloat16
F32 = jnp.float32
CAP = 2


def dot_nn(a, b):
    return jnp.dot(a, b, preferred_element_type=F32)


def dot_nt(a, b):
    return lax.dot_general(a, b, (((1,), (1,)), ((), ())), preferred_element_type=F32)


def dot_tn(a, b):
    return lax.dot_general(a, b, (((0,), (0,)), ((), ())), preferred_element_type=F32)


def iota(shape, dim):
    return lax.broadcasted_iota(jnp.int32, shape, dim).astype(F32)


def moe_kernel(
    n_dp, n_e,
    count_ref, ids_r, rep_r, prob_r, place_t,
    tokens_hbm, d_out_hbm, w_gate, w_up, w_down,
    layer_out, d_tokens, d_gates, g_gate, g_up, g_down,
    tokens, d_out,
    sel, pick0, pick1, wcol, prob_c,
    wg, wu, wd,
    a_send, x_recv, b_send, c_recv, o_recv, d_recv,
    xs, cot_sib, hs, h_sib, gs, us, r_send, r_mid, r_end,
    acc, gu_acc, gu_send, gu_recv,
    w_sem, t_sem,
    yz_send, yz_recv, fw_send, fw_recv, ag_send, ag_recv, pt_send, pt_recv,
    sib_send, sib_recv, ring_send, ring_recv,
):
    nx = n_dp // 2
    rows = n_dp * CAP
    slots = rows * n_e
    toks, width = tokens_hbm.shape
    chunk = width // nx
    half = chunk // 2
    acc_g, acc_u, acc_h = (acc.at[pl.ds(i * slots, slots)] for i in range(3))
    hid = w_down.shape[1]
    p = lax.axis_index("dp")
    e = lax.axis_index("expert")
    x = p // 2
    core = p % 2

    def at_x(d):
        return {"dp": lax.rem(x + d, nx) * 2 + core}

    sibling = {"dp": x * 2 + 1 - core}

    order = (2, 1, 3, 0)

    def away(j):
        if isinstance(j, int):
            return order[j]
        return jnp.where(j == 0, 2, jnp.where(j == 1, 1, jnp.where(j == 2, 3, 0)))

    def cols(j):
        return pl.ds(pl.multiple_of(lax.rem(x + away(j), nx) * chunk, chunk), chunk)

    barrier = pltpu.get_barrier_semaphore()

    def greet(d, _):
        pl.semaphore_signal(
            barrier, inc=1, device_id={"expert": lax.rem(e + d, n_e)}, device_id_type=MESH
        )
        return 0

    lax.fori_loop(1, n_e, greet, 0)
    for d in range(1, nx):
        pl.semaphore_signal(barrier, inc=1, device_id=at_x(d), device_id_type=MESH)
    pl.semaphore_signal(barrier, inc=1, device_id=sibling, device_id_type=MESH)

    def load_gate(j):
        return pltpu.make_async_copy(w_gate.at[0, cols(j)], wg.at[j], w_sem.at[0, j])

    def load_up(j):
        return pltpu.make_async_copy(w_up.at[0, cols(j)], wu.at[j], w_sem.at[1, j])

    def load_down(j):
        return pltpu.make_async_copy(w_down.at[0, :, cols(j)], wd.at[j], w_sem.at[2, j])

    def load_tok(j):
        return pltpu.make_async_copy(tokens_hbm.at[:, cols(j)], tokens.at[j], t_sem.at[0, j])

    def load_cot(j):
        return pltpu.make_async_copy(d_out_hbm.at[:, cols(j)], d_out.at[j], t_sem.at[1, j])

    for j in range(nx):
        load_tok(j).start()
    for j in range(nx):
        load_cot(j).start()
        load_gate(j).start()
        load_up(j).start()
    for j in range(nx):
        load_down(j).start()

    count = count_ref[0].astype(F32)
    place = place_t[...].astype(F32).astype(BF)
    tgt_r, dst_r, exp_r = [], [], []
    for k in range(2):
        er = ids_r[k : k + 1, :].astype(F32)
        rr = rep_r[k : k + 1, :].astype(F32)
        of_expert = jnp.where(iota((n_e, toks), 0) == er, 1.0, 0.0).astype(BF)
        holders = dot_nn(place, of_expert)
        dr = jnp.sum(jnp.where(iota((n_dp, toks), 0) == rr, holders, 0.0), axis=0, keepdims=True)
        exp_r.append(er)
        dst_r.append(dr)
        tgt_r.append(dr * n_e + er)
    t_sub = iota((toks, toks), 0)
    t_lane = iota((toks, toks), 1)
    diagonal = t_sub == t_lane

    def as_column(row):
        return jnp.sum(jnp.where(diagonal, row, 0.0), axis=1, keepdims=True)

    tgt_c = [as_column(tgt_r[k]) for k in range(2)]
    before = (t_sub < t_lane) & (t_sub < count)
    slot_r = []
    for k in range(2):
        rank = jnp.zeros((1, toks), F32)
        for m in range(2):
            rank += jnp.sum(
                jnp.where((tgt_c[m] == tgt_r[k]) & before, 1.0, 0.0), axis=0, keepdims=True
            )
        keep = (rank < CAP) & (iota((1, toks), 1) < count)
        slot_r.append(jnp.where(keep, exp_r[k] * rows + dst_r[k] * CAP + rank, -1.0))
    slot_sub = iota((slots, toks), 0)
    slot_lane = iota((toks, slots), 1)
    hit0 = slot_sub == slot_r[0]
    hit1 = slot_sub == slot_r[1]
    sel[...] = jnp.where(hit0 | hit1, 1.0, 0.0).astype(BF)
    wcol[...] = jnp.sum(
        jnp.where(hit0, prob_r[0:1, :], 0.0) + jnp.where(hit1, prob_r[1:2, :], 0.0),
        axis=1, keepdims=True,
    )

    def rest_of_routing():
        pick0[...] = jnp.where(slot_lane == as_column(slot_r[0]), 1.0, 0.0).astype(BF)
        pick1[...] = jnp.where(slot_lane == as_column(slot_r[1]), 1.0, 0.0).astype(BF)
        prob_c[0] = as_column(prob_r[0:1, :])
        prob_c[1] = as_column(prob_r[1:2, :])

    def block(i):
        return pl.ds(pl.multiple_of(i * rows, rows), rows)

    def exchange(stage, src, dst, j):
        def one(d, _):
            q = lax.rem(e + d, n_e)
            pltpu.make_async_remote_copy(
                src.at[j, block(q)], dst.at[j, block(e)],
                yz_send.at[stage, j], yz_recv.at[stage, j],
                device_id={"expert": q}, device_id_type=MESH,
            ).start()
            return 0

        lax.fori_loop(1, n_e, one, 0)
        pltpu.make_async_copy(
            src.at[j, block(e)], dst.at[j, block(e)], yz_recv.at[stage, j]
        ).start()

    def arrived(stage, dst, j):
        pltpu.make_async_copy(dst.at[j], dst.at[j], yz_recv.at[stage, j]).wait()

    def sent(stage, src, j):
        part = src.at[j, pl.ds(0, slots - rows)]
        pltpu.make_async_copy(part, part, yz_send.at[stage, j]).wait()

    def forward(j):
        return pltpu.make_async_remote_copy(
            x_recv.at[j], xs.at[j], fw_send.at[j], fw_recv.at[j],
            device_id=at_x(away(j)), device_id_type=MESH,
        )

    other = pl.multiple_of((1 - core) * half, half)
    mine = pl.multiple_of(core * half, half)

    def hidden_over():
        return pltpu.make_async_remote_copy(
            hs, h_sib, sib_send.at[nx], sib_recv.at[nx],
            device_id=sibling, device_id_type=MESH,
        )

    def cot_over(j):
        return pltpu.make_async_remote_copy(
            c_recv.at[j, :, pl.ds(other, half)], cot_sib.at[j], sib_send.at[j], sib_recv.at[j],
            device_id=sibling, device_id_type=MESH,
        )

    rcut = hid // 2

    def ring_half(way):
        r = pl.ds(way * rcut, rcut)
        return pltpu.make_async_remote_copy(
            r_send.at[0, r], r_mid.at[way], ring_send.at[way], ring_recv.at[way],
            device_id=at_x(1 if way == 0 else nx - 1), device_id_type=MESH,
        )

    def ring_whole(way):
        return pltpu.make_async_remote_copy(
            r_send.at[1 + way], r_end.at[way], ring_send.at[2 + way], ring_recv.at[2 + way],
            device_id=at_x(1 if way == 0 else nx - 1), device_id_type=MESH,
        )

    def down_part(j, start, size):
        c = pl.ds(start, size)
        m = pl.ds(pl.multiple_of(mine + start, size), size)
        return dot_tn(hs[...], c_recv[j, :, m]) + dot_tn(h_sib[...], cot_sib[j, :, c])

    cut = slots // 2

    def hand(which, buf, way):
        return pltpu.make_async_remote_copy(
            buf.at[0], buf.at[1 if way == 0 else nx - 1],
            ag_send.at[which, way], ag_recv.at[which, way],
            device_id=at_x(1 if way == 0 else nx - 1), device_id_type=MESH,
        )

    def relay(which, buf, way):
        r = pl.ds(way * cut, cut)
        return pltpu.make_async_remote_copy(
            buf.at[1 if way == 0 else nx - 1, r], buf.at[2, r],
            ag_send.at[which, 2 + way], ag_recv.at[which, 2 + way],
            device_id=at_x(1 if way == 0 else nx - 1), device_id_type=MESH,
        )

    def hand_out(which, buf):
        for way in (0, 1):
            hand(which, buf, way).start()

    def pass_on(which, buf):
        for way in (0, 1):
            hand(which, buf, way).wait_recv()
            relay(which, buf, way).start()

    def all_here(which, buf):
        for way in (0, 1):
            relay(which, buf, way).wait_recv()

    def gather_x(j):
        load_tok(j).wait()
        a_send[j] = dot_nn(sel[...], tokens[j]).astype(BF)

    gather_x(0)
    pl.semaphore_wait(barrier, n_e - 1 + nx - 1 + 1)
    exchange(0, a_send, x_recv, 0)

    def first(j, _):
        gather_x(j)

        @pl.when(j < 2)
        def _():
            exchange(0, a_send, x_recv, j)

        return 0

    lax.fori_loop(1, nx, first, 0)
    rest_of_routing()

    def gather_cot(j, _):
        load_cot(j).wait()
        raw = dot_nn(sel[...], d_out[j])
        b_send[j] = (raw * wcol[...]).astype(BF)
        return 0

    lax.fori_loop(0, nx, gather_cot, 0)

    acc_g[...] = jnp.zeros_like(acc_g)
    acc_u[...] = jnp.zeros_like(acc_u)
    acc_h[...] = jnp.zeros_like(acc_h)

    def pre_step(j, _):
        arrived(0, x_recv, j)

        @pl.when(j == 0)
        def _():
            for later in range(2, nx):
                exchange(0, a_send, x_recv, later)

        @pl.when(j > 0)
        def _():
            exchange(1, b_send, c_recv, j - 1)

        @pl.when(j == nx - 1)
        def _():
            exchange(1, b_send, c_recv, j)


        @pl.when(j < nx - 1)
        def _():
            forward(j).start()

        load_gate(j).wait()
        load_up(j).wait()
        acc_g[...] += dot_nn(x_recv[j], wg[j])
        acc_u[...] += dot_nn(x_recv[j], wu[j])
        return 0

    lax.fori_loop(0, nx, pre_step, 0)

    band = min(32, slots)

    def activate(i, _):
        r = pl.ds(pl.multiple_of(i * band, band), band)
        pre_g = acc_g[r, :]
        pre_u = acc_u[r, :]
        sig = jax.nn.sigmoid(pre_g)
        val = pre_g * sig
        hs[r, :] = (val * pre_u).astype(BF)
        acc_g[r, :] = pre_u * (sig * (1.0 + pre_g * (1.0 - sig)))
        acc_u[r, :] = val
        return 0

    lax.fori_loop(0, slots // band, activate, 0)
    hidden_over().start()

    tile = half // 2
    tiles = [(t * tile, pl.ds(t * tile, tile)) for t in range(half // tile)]

    def cot_step(j, _):
        arrived(1, c_recv, j)
        cot_over(j).start()
        load_down(j).wait()
        sent(0, a_send, j)
        a_send[j] = dot_nn(hs[...], wd[j]).astype(BF)
        exchange(2, a_send, o_recv, j)
        acc_h[...] += dot_nt(c_recv[j], wd[j])
        return 0

    cot_step(0, 0)
    hidden_over().wait_recv()
    cot_over(0).wait_recv()
    for start, r in tiles:
        r_send[0, :, r] = down_part(0, start, tile).astype(BF)
    for way in (0, 1):
        ring_half(way).start()
    for way in (0, 1):
        cot_step(1 + way, 0)
        cot_over(1 + way).wait_recv()
        ring_half(way).wait_recv()
        part = pl.ds(way * rcut, rcut)
        rest = pl.ds((1 - way) * rcut, rcut)
        for start, r in tiles:
            value = down_part(1 + way, start, tile)
            with_mid = value[way * rcut : (way + 1) * rcut] + r_mid[way, :, r].astype(F32)
            r_send[1 + way, part, r] = with_mid.astype(BF)
            r_send[1 + way, rest, r] = value[(1 - way) * rcut : (2 - way) * rcut].astype(BF)
        ring_whole(way).start()
    cot_step(nx - 1, 0)

    def slopes(i, _):
        r = pl.ds(pl.multiple_of(i * band, band), band)
        d_h = acc_h[r, :]
        gs[0, r, :] = (d_h * acc_g[r, :]).astype(BF)
        us[0, r, :] = (d_h * acc_u[r, :]).astype(BF)
        return 0

    lax.fori_loop(0, slots // band, slopes, 0)
    hand_out(0, gs)
    hand_out(1, us)

    def dx_step(j, _):
        sent(1, b_send, j)
        b_send[j] = (dot_nt(gs[0], wg[j]) + dot_nt(us[0], wu[j])).astype(BF)
        exchange(3, b_send, d_recv, j)
        return 0

    lax.fori_loop(0, nx, dx_step, 0)

    def out_step(j, carry):
        g0, g1 = carry
        arrived(2, o_recv, j)
        got = o_recv[j]
        out0 = dot_nn(pick0[...], got)
        out1 = dot_nn(pick1[...], got)
        cot = d_out[j].astype(F32)
        layer_out[:, cols(j)] = (prob_c[0] * out0 + prob_c[1] * out1).astype(BF)
        g0 = g0 + jnp.sum(cot * out0, axis=1, keepdims=True)
        g1 = g1 + jnp.sum(cot * out1, axis=1, keepdims=True)
        return g0, g1

    zero = jnp.zeros((toks, 1), F32)
    carry = lax.fori_loop(0, nx - 2, out_step, (zero, zero))
    pass_on(0, gs)
    carry = out_step(nx - 2, carry)
    pass_on(1, us)
    g0, g1 = out_step(nx - 1, carry)

    def as_row(column):
        return jnp.sum(jnp.where(diagonal, column, 0.0), axis=0, keepdims=True)

    d_gates[0:1, :] = as_row(g0)
    d_gates[1:2, :] = as_row(g1)

    def row_block(d):
        if d == 0:
            return x_recv.at[nx - 1]
        return xs.at[order.index(d)]

    def grad_tile(which, start, blocks):
        c = pl.ds(pl.multiple_of(start, tile), tile)
        total = None
        for d in blocks:
            term = dot_tn(row_block(d)[:, c], (gs, us)[which][d])
            total = term if total is None else total + term
        return total

    def part_copy(which):
        return pltpu.make_async_remote_copy(
            gu_send.at[which], gu_recv.at[which], pt_send.at[which], pt_recv.at[which],
            device_id=sibling, device_id_type=MESH,
        )

    near_blocks = [0, 1, nx - 1]

    def first_blocks(which):
        for start, r in tiles:
            gu_acc[which, 0, r, :] = grad_tile(which, other + start, near_blocks)
            gu_acc[which, 1, r, :] = grad_tile(which, mine + start, near_blocks)

    def last_block(which):
        all_here(which, (gs, us)[which])
        for start, r in tiles:
            last = grad_tile(which, other + start, [2])
            gu_send[which, r, :] = (gu_acc[which, 0, r, :] + last).astype(BF)
        part_copy(which).start()
        for start, r in tiles:
            gu_acc[which, 1, r, :] += grad_tile(which, mine + start, [2])

    def finish(which):
        part_copy(which).wait_recv()
        (g_gate, g_up)[which][0] = (
            gu_acc[which, 1] + gu_recv[which].astype(F32)
        ).astype(BF)

    def finish_down():
        for way in (0, 1):
            ring_whole(way).wait_recv()
        cot_over(nx - 1).wait_recv()
        for start, r in tiles:
            value = down_part(nx - 1, start, tile)
            value += r_end[0, :, r].astype(F32) + r_end[1, :, r].astype(F32)
            g_down[0, :, r] = value.astype(BF)

    def tok_step(j):
        arrived(3, d_recv, j)
        d_tokens[:, cols(j)] = dot_nn(pick0[...] + pick1[...], d_recv[j]).astype(BF)

    for j in range(nx - 1):
        forward(j).wait_recv()
    first_blocks(0)
    first_blocks(1)
    finish_down()
    tok_step(0)
    last_block(0)
    tok_step(1)
    last_block(1)
    finish(0)
    tok_step(2)
    finish(1)
    tok_step(3)

    for which in (0, 1):
        part_copy(which).wait_send()

    def drain(j, _):
        sent(2, a_send, j)
        sent(3, b_send, j)
        return 0

    lax.fori_loop(0, nx, drain, 0)
    for j in range(nx - 1):
        forward(j).wait_send()
    for j in range(nx):
        cot_over(j).wait_send()
    hidden_over().wait_send()
    for way in (0, 1):
        ring_half(way).wait_send()
        ring_whole(way).wait_send()
    for which, buf in enumerate((gs, us)):
        for way in (0, 1):
            hand(which, buf, way).wait_send()
            relay(which, buf, way).wait_send()


def place_kernel(*refs):
    n = (len(refs) - 1) // 2
    copies = [pltpu.make_async_copy(refs[i], refs[n + i], refs[-1].at[i]) for i in range(n)]
    for copy in copies:
        copy.start()
    for copy in copies:
        copy.wait()


def on_device(
    tokens, gate_probs, expert_ids, placement, replica, row_counts, w_gate, w_up, w_down, d_out
):
    n_dp = lax.axis_size("dp")
    n_e = lax.axis_size("expert")
    nx = n_dp // 2
    toks, width = tokens.shape
    hid = w_gate.shape[2]
    slots = n_dp * CAP * n_e
    chunk = width // nx
    half = chunk // 2
    vmem = pl.BlockSpec(memory_space=pltpu.VMEM)
    hbm = pl.BlockSpec(memory_space=pl.ANY)
    smem = pl.BlockSpec(memory_space=pltpu.SMEM)
    yz = (nx, slots, chunk)
    near = (nx - 1, slots, chunk)
    wide = (nx, slots, hid)
    dma = pltpu.SemaphoreType.DMA
    flops = 18 * slots * width * hid
    outs = (
        jax.ShapeDtypeStruct((toks, width), BF),
        jax.ShapeDtypeStruct((toks, width), BF),
        jax.ShapeDtypeStruct((2, toks), F32),
        jax.ShapeDtypeStruct((1, half, hid), BF),
        jax.ShapeDtypeStruct((1, half, hid), BF),
        jax.ShapeDtypeStruct((1, hid, half), BF),
    )
    mine = (nx, toks, chunk)
    results = pl.pallas_call(
        functools.partial(moe_kernel, n_dp, n_e),
        out_shape=[pltpu.VMEM(out.shape, out.dtype) for out in outs],
        in_specs=[smem] + [vmem] * 4 + [hbm] * 5,
        out_specs=[vmem] * 6,
        scratch_shapes=[
            pltpu.VMEM(mine, BF),
            pltpu.VMEM(mine, BF),
            pltpu.VMEM((slots, toks), BF),
            pltpu.VMEM((toks, slots), BF),
            pltpu.VMEM((toks, slots), BF),
            pltpu.VMEM((slots, 1), F32),
            pltpu.VMEM((2, toks, 1), F32),
            pltpu.VMEM((nx, chunk, hid), BF),
            pltpu.VMEM((nx, chunk, hid), BF),
            pltpu.VMEM((nx, hid, chunk), BF),
            pltpu.VMEM(yz, BF),
            pltpu.VMEM(yz, BF),
            pltpu.VMEM(yz, BF),
            pltpu.VMEM(yz, BF),
            pltpu.VMEM(yz, BF),
            pltpu.VMEM(yz, BF),
            pltpu.VMEM(near, BF),
            pltpu.VMEM((nx, slots, half), BF),
            pltpu.VMEM((slots, hid), BF),
            pltpu.VMEM((slots, hid), BF),
            pltpu.VMEM(wide, BF),
            pltpu.VMEM(wide, BF),
            pltpu.VMEM((3, hid, half), BF),
            pltpu.VMEM((2, hid // 2, half), BF),
            pltpu.VMEM((2, hid, half), BF),
            pltpu.VMEM((3 * slots, hid), F32),
            pltpu.VMEM((2, 2, half, hid), F32),
            pltpu.VMEM((2, half, hid), BF),
            pltpu.VMEM((2, half, hid), BF),
            dma((3, nx)),
            dma((2, nx)),
            dma((4, nx)),
            dma((4, nx)),
            dma((nx - 1,)),
            dma((nx - 1,)),
            dma((2, 4)),
            dma((2, 4)),
            dma((2,)),
            dma((2,)),
            dma((nx + 1,)),
            dma((nx + 1,)),
            dma((4,)),
            dma((4,)),
        ],
        compiler_params=pltpu.CompilerParams(
            collective_id=0, has_side_effects=True, vmem_limit_bytes=58 << 20
        ),
        cost_estimate=pl.CostEstimate(flops=flops, bytes_accessed=6 * width * hid, transcendentals=0),
        name="moe",
    )(
        row_counts, expert_ids.T, replica.T, gate_probs.T, placement.T,
        tokens, d_out, w_gate, w_up, w_down,
    )
    results = pl.pallas_call(
        place_kernel,
        out_shape=outs,
        in_specs=[hbm] * 6,
        out_specs=[hbm] * 6,
        scratch_shapes=[dma((6,))],
        compiler_params=pltpu.CompilerParams(vmem_limit_bytes=1 << 20),
        name="place",
    )(*[pltpu.with_memory_space_constraint(result, pltpu.VMEM) for result in results])
    layer_out, d_tokens, d_gates, g_gate, g_up, g_down = results
    return layer_out, d_tokens, d_gates.T, g_gate, g_up, g_down


def solution(mesh):
    rows = P(("dp", "expert"), None)
    weight = P("expert", None, None)
    return jax.shard_map(
        on_device,
        mesh=mesh,
        in_specs=(
            rows, rows, rows, P(), rows, P(("dp", "expert")), weight, weight, weight, rows,
        ),
        out_specs=(
            rows, rows, rows,
            P("expert", "dp", None), P("expert", "dp", None), P("expert", None, "dp"),
        ),
        check_vma=False,
    )
```

```python
import functools

import jax
import jax.numpy as jnp
from jax import lax
from jax.experimental import pallas as pl
from jax.experimental.pallas import tpu as pltpu
from jax.sharding import PartitionSpec as P

MESH = pl.DeviceIdType.MESH
BF = jnp.bfloat16
F32 = jnp.float32
CAP = 2


def dot_nn(a, b):
    return jnp.dot(a, b, preferred_element_type=F32)


def dot_nt(a, b):
    return lax.dot_general(a, b, (((1,), (1,)), ((), ())), preferred_element_type=F32)


def dot_tn(a, b):
    return lax.dot_general(a, b, (((0,), (0,)), ((), ())), preferred_element_type=F32)


def iota(shape, dim):
    return lax.broadcasted_iota(jnp.int32, shape, dim).astype(F32)


def moe_kernel(
    n_dp, n_e,
    count_hbm, ids_hbm, rep_hbm, prob_hbm, place_hbm,
    tokens_hbm, d_out_hbm, w_gate, w_up, w_down,
    layer_out, d_tokens, d_gates, g_gate, g_up, g_down,
    count_ref, ids_r, rep_r, prob_r, place_t,
    tokens, d_out,
    sel, pick0, pick1, wcol, prob_c,
    wg, wu, wd,
    a_send, x_recv, b_send, c_recv, o_recv, d_recv,
    xs, cot_sib, hs, h_sib, gs, us, r_send, r_mid, r_end,
    acc, gu_acc, gu_send, gu_recv,
    s_sem, w_sem, t_sem,
    yz_send, yz_recv, fw_send, fw_recv, ag_send, ag_recv, pt_send, pt_recv,
    sib_send, sib_recv, ring_send, ring_recv,
):
    nx = n_dp // 2
    rows = n_dp * CAP
    slots = rows * n_e
    toks, width = tokens_hbm.shape
    chunk = width // nx
    half = chunk // 2
    acc_g, acc_u, acc_h = (acc.at[pl.ds(i * slots, slots)] for i in range(3))
    hid = w_down.shape[1]
    p = lax.axis_index("dp")
    e = lax.axis_index("expert")
    x = p // 2
    core = p % 2

    def at_x(d):
        return {"dp": lax.rem(x + d, nx) * 2 + core}

    sibling = {"dp": x * 2 + 1 - core}

    order = (2, 1, 3, 0)

    def away(j):
        if isinstance(j, int):
            return order[j]
        return jnp.where(j == 0, 2, jnp.where(j == 1, 1, jnp.where(j == 2, 3, 0)))

    def cols(j):
        return pl.ds(pl.multiple_of(lax.rem(x + away(j), nx) * chunk, chunk), chunk)

    small = [
        pltpu.make_async_copy(src, dst, s_sem.at[i])
        for i, (src, dst) in enumerate((
            (ids_hbm, ids_r), (rep_hbm, rep_r), (place_hbm, place_t),
            (count_hbm, count_ref), (prob_hbm, prob_r),
        ))
    ]
    for copy in small:
        copy.start()

    barrier = pltpu.get_barrier_semaphore()

    def greet(d, _):
        pl.semaphore_signal(
            barrier, inc=1, device_id={"expert": lax.rem(e + d, n_e)}, device_id_type=MESH
        )
        return 0

    lax.fori_loop(1, n_e, greet, 0)
    for d in range(1, nx):
        pl.semaphore_signal(barrier, inc=1, device_id=at_x(d), device_id_type=MESH)
    pl.semaphore_signal(barrier, inc=1, device_id=sibling, device_id_type=MESH)

    def load_gate(j):
        return pltpu.make_async_copy(w_gate.at[0, cols(j)], wg.at[j], w_sem.at[0, j])

    def load_up(j):
        return pltpu.make_async_copy(w_up.at[0, cols(j)], wu.at[j], w_sem.at[1, j])

    def load_down(j):
        return pltpu.make_async_copy(w_down.at[0, :, cols(j)], wd.at[j], w_sem.at[2, j])

    def load_tok(j):
        return pltpu.make_async_copy(tokens_hbm.at[:, cols(j)], tokens.at[j], t_sem.at[0, j])

    def load_cot(j):
        return pltpu.make_async_copy(d_out_hbm.at[:, cols(j)], d_out.at[j], t_sem.at[1, j])

    for j in range(nx):
        load_tok(j).start()
    for j in range(nx):
        load_cot(j).start()
        load_gate(j).start()
        load_up(j).start()
    for j in range(nx):
        load_down(j).start()

    for copy in small:
        copy.wait()
    count = count_ref[0].astype(F32)
    place = place_t[...].astype(F32).astype(BF)
    tgt_r, dst_r, exp_r = [], [], []
    for k in range(2):
        er = ids_r[k : k + 1, :].astype(F32)
        rr = rep_r[k : k + 1, :].astype(F32)
        of_expert = jnp.where(iota((n_e, toks), 0) == er, 1.0, 0.0).astype(BF)
        holders = dot_nn(place, of_expert)
        dr = jnp.sum(jnp.where(iota((n_dp, toks), 0) == rr, holders, 0.0), axis=0, keepdims=True)
        exp_r.append(er)
        dst_r.append(dr)
        tgt_r.append(dr * n_e + er)
    t_sub = iota((toks, toks), 0)
    t_lane = iota((toks, toks), 1)
    diagonal = t_sub == t_lane

    def as_column(row):
        return jnp.sum(jnp.where(diagonal, row, 0.0), axis=1, keepdims=True)

    tgt_c = [as_column(tgt_r[k]) for k in range(2)]
    before = (t_sub < t_lane) & (t_sub < count)
    slot_r = []
    for k in range(2):
        rank = jnp.zeros((1, toks), F32)
        for m in range(2):
            rank += jnp.sum(
                jnp.where((tgt_c[m] == tgt_r[k]) & before, 1.0, 0.0), axis=0, keepdims=True
            )
        keep = (rank < CAP) & (iota((1, toks), 1) < count)
        slot_r.append(jnp.where(keep, exp_r[k] * rows + dst_r[k] * CAP + rank, -1.0))
    slot_sub = iota((slots, toks), 0)
    slot_lane = iota((toks, slots), 1)
    hit0 = slot_sub == slot_r[0]
    hit1 = slot_sub == slot_r[1]
    sel[...] = jnp.where(hit0 | hit1, 1.0, 0.0).astype(BF)

    def rest_of_routing():
        wcol[...] = jnp.sum(
            jnp.where(hit0, prob_r[0:1, :], 0.0) + jnp.where(hit1, prob_r[1:2, :], 0.0),
            axis=1, keepdims=True,
        )
        pick0[...] = jnp.where(slot_lane == as_column(slot_r[0]), 1.0, 0.0).astype(BF)
        pick1[...] = jnp.where(slot_lane == as_column(slot_r[1]), 1.0, 0.0).astype(BF)
        prob_c[0] = as_column(prob_r[0:1, :])
        prob_c[1] = as_column(prob_r[1:2, :])

    side = 4

    def block(i):
        return pl.ds(pl.multiple_of(i * rows, rows), rows)

    def exchange(stage, src, dst, j):
        def one(d, _):
            q = lax.rem(e // side + d // side, side) * side + lax.rem(e % side + d % side, side)
            pltpu.make_async_remote_copy(
                src.at[j, block(q)], dst.at[j, block(e)],
                yz_send.at[stage, j], yz_recv.at[stage, j],
                device_id={"expert": q}, device_id_type=MESH,
            ).start()
            return 0

        lax.fori_loop(1, n_e, one, 0)
        pltpu.make_async_copy(
            src.at[j, block(e)], dst.at[j, block(e)], yz_recv.at[stage, j]
        ).start()

    def arrived(stage, dst, j):
        pltpu.make_async_copy(dst.at[j], dst.at[j], yz_recv.at[stage, j]).wait()

    def sent(stage, src, j):
        part = src.at[j, pl.ds(0, slots - rows)]
        pltpu.make_async_copy(part, part, yz_send.at[stage, j]).wait()

    def forward(j):
        return pltpu.make_async_remote_copy(
            x_recv.at[j], xs.at[j], fw_send.at[j], fw_recv.at[j],
            device_id=at_x(away(j)), device_id_type=MESH,
        )

    other = pl.multiple_of((1 - core) * half, half)
    mine = pl.multiple_of(core * half, half)

    def hidden_over():
        return pltpu.make_async_remote_copy(
            hs, h_sib, sib_send.at[nx], sib_recv.at[nx],
            device_id=sibling, device_id_type=MESH,
        )

    def cot_over(j):
        return pltpu.make_async_remote_copy(
            c_recv.at[j, :, pl.ds(other, half)], cot_sib.at[j], sib_send.at[j], sib_recv.at[j],
            device_id=sibling, device_id_type=MESH,
        )

    rcut = hid // 2

    def ring_half(way):
        r = pl.ds(way * rcut, rcut)
        return pltpu.make_async_remote_copy(
            r_send.at[0, r], r_mid.at[way], ring_send.at[way], ring_recv.at[way],
            device_id=at_x(1 if way == 0 else nx - 1), device_id_type=MESH,
        )

    def ring_whole(way):
        return pltpu.make_async_remote_copy(
            r_send.at[1 + way], r_end.at[way], ring_send.at[2 + way], ring_recv.at[2 + way],
            device_id=at_x(1 if way == 0 else nx - 1), device_id_type=MESH,
        )

    def down_part(j, start, size):
        c = pl.ds(start, size)
        m = pl.ds(pl.multiple_of(mine + start, size), size)
        return dot_tn(hs[...], c_recv[j, :, m]) + dot_tn(h_sib[...], cot_sib[j, :, c])

    cut = slots // 2

    def hand(which, buf, way):
        return pltpu.make_async_remote_copy(
            buf.at[0], buf.at[1 if way == 0 else nx - 1],
            ag_send.at[which, way], ag_recv.at[which, way],
            device_id=at_x(1 if way == 0 else nx - 1), device_id_type=MESH,
        )

    def relay(which, buf, way):
        r = pl.ds(way * cut, cut)
        return pltpu.make_async_remote_copy(
            buf.at[1 if way == 0 else nx - 1, r], buf.at[2, r],
            ag_send.at[which, 2 + way], ag_recv.at[which, 2 + way],
            device_id=at_x(1 if way == 0 else nx - 1), device_id_type=MESH,
        )

    def hand_out(which, buf):
        for way in (0, 1):
            hand(which, buf, way).start()

    def pass_on(which, buf):
        for way in (0, 1):
            hand(which, buf, way).wait_recv()
            relay(which, buf, way).start()

    def all_here(which, buf):
        for way in (0, 1):
            relay(which, buf, way).wait_recv()

    def gather_x(j):
        load_tok(j).wait()
        a_send[j] = dot_nn(sel[...], tokens[j]).astype(BF)

    gather_x(0)
    pl.semaphore_wait(barrier, n_e - 1 + nx - 1 + 1)
    exchange(0, a_send, x_recv, 0)

    def first(j, _):
        gather_x(j)

        @pl.when(j < 2)
        def _():
            exchange(0, a_send, x_recv, j)

        return 0

    lax.fori_loop(1, nx, first, 0)
    rest_of_routing()

    def gather_cot(j, _):
        load_cot(j).wait()
        raw = dot_nn(sel[...], d_out[j])
        b_send[j] = (raw * wcol[...]).astype(BF)
        return 0

    lax.fori_loop(0, nx, gather_cot, 0)

    acc_g[...] = jnp.zeros_like(acc_g)
    acc_u[...] = jnp.zeros_like(acc_u)
    acc_h[...] = jnp.zeros_like(acc_h)

    def pre_step(j, _):
        arrived(0, x_recv, j)

        @pl.when(j == 0)
        def _():
            for later in range(2, nx):
                exchange(0, a_send, x_recv, later)

        @pl.when(j > 0)
        def _():
            exchange(1, b_send, c_recv, j - 1)

        @pl.when(j == nx - 1)
        def _():
            exchange(1, b_send, c_recv, j)


        @pl.when(j < nx - 1)
        def _():
            forward(j).start()

        load_gate(j).wait()
        load_up(j).wait()
        acc_g[...] += dot_nn(x_recv[j], wg[j])
        acc_u[...] += dot_nn(x_recv[j], wu[j])
        return 0

    lax.fori_loop(0, nx, pre_step, 0)

    band = min(32, slots)

    def activate(i, _):
        r = pl.ds(pl.multiple_of(i * band, band), band)
        pre_g = acc_g[r, :]
        pre_u = acc_u[r, :]
        sig = jax.nn.sigmoid(pre_g)
        val = pre_g * sig
        hs[r, :] = (val * pre_u).astype(BF)
        acc_g[r, :] = pre_u * (sig * (1.0 + pre_g * (1.0 - sig)))
        acc_u[r, :] = val
        return 0

    lax.fori_loop(0, slots // band, activate, 0)
    hidden_over().start()

    tile = half // 2
    tiles = [(t * tile, pl.ds(t * tile, tile)) for t in range(half // tile)]

    def cot_step(j, _):
        arrived(1, c_recv, j)
        cot_over(j).start()
        load_down(j).wait()
        sent(0, a_send, j)
        a_send[j] = dot_nn(hs[...], wd[j]).astype(BF)
        exchange(2, a_send, o_recv, j)
        acc_h[...] += dot_nt(c_recv[j], wd[j])
        return 0

    cot_step(0, 0)
    hidden_over().wait_recv()
    cot_over(0).wait_recv()
    for start, r in tiles:
        r_send[0, :, r] = down_part(0, start, tile).astype(BF)
    for way in (0, 1):
        ring_half(way).start()
    cot_step(1, 0)
    cot_step(2, 0)
    for way in (0, 1):
        cot_over(1 + way).wait_recv()
        ring_half(way).wait_recv()
        part = pl.ds(way * rcut, rcut)
        rest = pl.ds((1 - way) * rcut, rcut)
        for start, r in tiles:
            value = down_part(1 + way, start, tile)
            with_mid = value[way * rcut : (way + 1) * rcut] + r_mid[way, :, r].astype(F32)
            r_send[1 + way, part, r] = with_mid.astype(BF)
            r_send[1 + way, rest, r] = value[(1 - way) * rcut : (2 - way) * rcut].astype(BF)
        ring_whole(way).start()
    cot_step(nx - 1, 0)

    def slopes(i, _):
        r = pl.ds(pl.multiple_of(i * band, band), band)
        d_h = acc_h[r, :]
        gs[0, r, :] = (d_h * acc_g[r, :]).astype(BF)
        us[0, r, :] = (d_h * acc_u[r, :]).astype(BF)
        return 0

    lax.fori_loop(0, slots // band, slopes, 0)
    hand_out(0, gs)
    hand_out(1, us)

    def dx_step(j, _):
        sent(1, b_send, j)
        b_send[j] = (dot_nt(gs[0], wg[j]) + dot_nt(us[0], wu[j])).astype(BF)
        exchange(3, b_send, d_recv, j)
        return 0

    lax.fori_loop(0, nx, dx_step, 0)

    def out_step(j, carry):
        g0, g1 = carry
        arrived(2, o_recv, j)
        got = o_recv[j]
        out0 = dot_nn(pick0[...], got)
        out1 = dot_nn(pick1[...], got)
        cot = d_out[j].astype(F32)
        layer_out[:, cols(j)] = (prob_c[0] * out0 + prob_c[1] * out1).astype(BF)
        g0 = g0 + jnp.sum(cot * out0, axis=1, keepdims=True)
        g1 = g1 + jnp.sum(cot * out1, axis=1, keepdims=True)
        return g0, g1

    zero = jnp.zeros((toks, 1), F32)
    carry = lax.fori_loop(0, nx - 2, out_step, (zero, zero))
    pass_on(0, gs)
    carry = out_step(nx - 2, carry)
    pass_on(1, us)
    g0, g1 = out_step(nx - 1, carry)

    def as_row(column):
        return jnp.sum(jnp.where(diagonal, column, 0.0), axis=0, keepdims=True)

    d_gates[0:1, :] = as_row(g0)
    d_gates[1:2, :] = as_row(g1)

    def row_block(d):
        if d == 0:
            return x_recv.at[nx - 1]
        return xs.at[order.index(d)]

    def grad_tile(which, start, blocks):
        c = pl.ds(pl.multiple_of(start, tile), tile)
        total = None
        for d in blocks:
            term = dot_tn(row_block(d)[:, c], (gs, us)[which][d])
            total = term if total is None else total + term
        return total

    def part_copy(which):
        return pltpu.make_async_remote_copy(
            gu_send.at[which], gu_recv.at[which], pt_send.at[which], pt_recv.at[which],
            device_id=sibling, device_id_type=MESH,
        )

    near_blocks = [0, 1, nx - 1]

    def first_blocks(which):
        for start, r in tiles:
            gu_acc[which, 0, r, :] = grad_tile(which, other + start, near_blocks)
            gu_acc[which, 1, r, :] = grad_tile(which, mine + start, near_blocks)

    def last_block(which):
        all_here(which, (gs, us)[which])
        for start, r in tiles:
            last = grad_tile(which, other + start, [2])
            gu_send[which, r, :] = (gu_acc[which, 0, r, :] + last).astype(BF)
        part_copy(which).start()
        for start, r in tiles:
            gu_acc[which, 1, r, :] += grad_tile(which, mine + start, [2])

    def finish(which):
        part_copy(which).wait_recv()
        (g_gate, g_up)[which][0] = (
            gu_acc[which, 1] + gu_recv[which].astype(F32)
        ).astype(BF)

    def finish_down():
        for way in (0, 1):
            ring_whole(way).wait_recv()
        cot_over(nx - 1).wait_recv()
        for start, r in tiles:
            value = down_part(nx - 1, start, tile)
            value += r_end[0, :, r].astype(F32) + r_end[1, :, r].astype(F32)
            g_down[0, :, r] = value.astype(BF)

    def tok_step(j):
        arrived(3, d_recv, j)
        d_tokens[:, cols(j)] = dot_nn(pick0[...] + pick1[...], d_recv[j]).astype(BF)

    for j in range(nx - 1):
        forward(j).wait_recv()
    first_blocks(0)
    first_blocks(1)
    finish_down()
    tok_step(0)
    last_block(0)
    tok_step(1)
    last_block(1)
    finish(0)
    tok_step(2)
    finish(1)
    tok_step(3)

    for which in (0, 1):
        part_copy(which).wait_send()

    def drain(j, _):
        sent(2, a_send, j)
        sent(3, b_send, j)
        return 0

    lax.fori_loop(0, nx, drain, 0)
    for j in range(nx - 1):
        forward(j).wait_send()
    for j in range(nx):
        cot_over(j).wait_send()
    hidden_over().wait_send()
    for way in (0, 1):
        ring_half(way).wait_send()
        ring_whole(way).wait_send()
    for which, buf in enumerate((gs, us)):
        for way in (0, 1):
            hand(which, buf, way).wait_send()
            relay(which, buf, way).wait_send()


def place_kernel(*refs):
    n = (len(refs) - 1) // 2
    copies = [pltpu.make_async_copy(refs[i], refs[n + i], refs[-1].at[i]) for i in range(n)]
    for copy in copies:
        copy.start()
    for copy in copies:
        copy.wait()


def on_device(
    tokens, gate_probs, expert_ids, placement, replica, row_counts, w_gate, w_up, w_down, d_out
):
    n_dp = lax.axis_size("dp")
    n_e = lax.axis_size("expert")
    nx = n_dp // 2
    toks, width = tokens.shape
    hid = w_gate.shape[2]
    slots = n_dp * CAP * n_e
    chunk = width // nx
    half = chunk // 2
    vmem = pl.BlockSpec(memory_space=pltpu.VMEM)
    hbm = pl.BlockSpec(memory_space=pl.ANY)
    yz = (nx, slots, chunk)
    near = (nx - 1, slots, chunk)
    wide = (nx, slots, hid)
    dma = pltpu.SemaphoreType.DMA
    flops = 18 * slots * width * hid
    outs = (
        jax.ShapeDtypeStruct((toks, width), BF),
        jax.ShapeDtypeStruct((toks, width), BF),
        jax.ShapeDtypeStruct((2, toks), F32),
        jax.ShapeDtypeStruct((1, half, hid), BF),
        jax.ShapeDtypeStruct((1, half, hid), BF),
        jax.ShapeDtypeStruct((1, hid, half), BF),
    )
    mine = (nx, toks, chunk)
    results = pl.pallas_call(
        functools.partial(moe_kernel, n_dp, n_e),
        out_shape=[pltpu.VMEM(out.shape, out.dtype) for out in outs],
        in_specs=[hbm] * 10,
        out_specs=[vmem] * 6,
        scratch_shapes=[
            pltpu.SMEM((1,), jnp.int32),
            pltpu.VMEM((2, toks), jnp.int32),
            pltpu.VMEM((2, toks), jnp.int32),
            pltpu.VMEM((2, toks), F32),
            pltpu.VMEM((n_dp, n_e), jnp.int32),
            pltpu.VMEM(mine, BF),
            pltpu.VMEM(mine, BF),
            pltpu.VMEM((slots, toks), BF),
            pltpu.VMEM((toks, slots), BF),
            pltpu.VMEM((toks, slots), BF),
            pltpu.VMEM((slots, 1), F32),
            pltpu.VMEM((2, toks, 1), F32),
            pltpu.VMEM((nx, chunk, hid), BF),
            pltpu.VMEM((nx, chunk, hid), BF),
            pltpu.VMEM((nx, hid, chunk), BF),
            pltpu.VMEM(yz, BF),
            pltpu.VMEM(yz, BF),
            pltpu.VMEM(yz, BF),
            pltpu.VMEM(yz, BF),
            pltpu.VMEM(yz, BF),
            pltpu.VMEM(yz, BF),
            pltpu.VMEM(near, BF),
            pltpu.VMEM((nx, slots, half), BF),
            pltpu.VMEM((slots, hid), BF),
            pltpu.VMEM((slots, hid), BF),
            pltpu.VMEM(wide, BF),
            pltpu.VMEM(wide, BF),
            pltpu.VMEM((3, hid, half), BF),
            pltpu.VMEM((2, hid // 2, half), BF),
            pltpu.VMEM((2, hid, half), BF),
            pltpu.VMEM((3 * slots, hid), F32),
            pltpu.VMEM((2, 2, half, hid), F32),
            pltpu.VMEM((2, half, hid), BF),
            pltpu.VMEM((2, half, hid), BF),
            dma((5,)),
            dma((3, nx)),
            dma((2, nx)),
            dma((4, nx)),
            dma((4, nx)),
            dma((nx - 1,)),
            dma((nx - 1,)),
            dma((2, 4)),
            dma((2, 4)),
            dma((2,)),
            dma((2,)),
            dma((nx + 1,)),
            dma((nx + 1,)),
            dma((4,)),
            dma((4,)),
        ],
        compiler_params=pltpu.CompilerParams(
            collective_id=0, has_side_effects=True, vmem_limit_bytes=58 << 20
        ),
        cost_estimate=pl.CostEstimate(flops=flops, bytes_accessed=6 * width * hid, transcendentals=0),
        name="moe",
    )(
        row_counts, expert_ids.T, replica.T, gate_probs.T, placement.T,
        tokens, d_out, w_gate, w_up, w_down,
    )
    results = pl.pallas_call(
        place_kernel,
        out_shape=outs,
        in_specs=[hbm] * 6,
        out_specs=[hbm] * 6,
        scratch_shapes=[dma((6,))],
        compiler_params=pltpu.CompilerParams(vmem_limit_bytes=1 << 20),
        name="place",
    )(*[pltpu.with_memory_space_constraint(result, pltpu.VMEM) for result in results])
    layer_out, d_tokens, d_gates, g_gate, g_up, g_down = results
    return layer_out, d_tokens, d_gates.T, g_gate, g_up, g_down


def solution(mesh):
    rows = P(("dp", "expert"), None)
    weight = P("expert", None, None)
    return jax.shard_map(
        on_device,
        mesh=mesh,
        in_specs=(
            rows, rows, rows, P(), rows, P(("dp", "expert")), weight, weight, weight, rows,
        ),
        out_specs=(
            rows, rows, rows,
            P("expert", "dp", None), P("expert", "dp", None), P("expert", None, "dp"),
        ),
        check_vma=False,
    )
```

```python
import functools

import jax
import jax.numpy as jnp
from jax import lax
from jax.experimental import pallas as pl
from jax.experimental.pallas import tpu as pltpu
from jax.sharding import PartitionSpec as P

MESH = pl.DeviceIdType.MESH
BF = jnp.bfloat16
F32 = jnp.float32
CAP = 2


def dot_nn(a, b):
    return jnp.dot(a, b, preferred_element_type=F32)


def dot_nt(a, b):
    return lax.dot_general(a, b, (((1,), (1,)), ((), ())), preferred_element_type=F32)


def dot_tn(a, b):
    return lax.dot_general(a, b, (((0,), (0,)), ((), ())), preferred_element_type=F32)


def iota(shape, dim):
    return lax.broadcasted_iota(jnp.int32, shape, dim).astype(F32)


def moe_kernel(
    n_dp, n_e,
    count_hbm, ids_hbm, rep_hbm, prob_hbm, place_hbm,
    tokens_hbm, d_out_hbm, w_gate, w_up, w_down,
    layer_out, d_tokens, d_gates, g_gate, g_up, g_down,
    count_ref, ids_r, rep_r, prob_r, place_t,
    tokens, d_out,
    sel, pick0, pick1, wcol, prob_c,
    wg, wu, wd,
    a_send, x_recv, b_send, c_recv, o_recv, d_recv,
    xs, cot_sib, hs, h_sib, gs, us, r_send, r_mid, r_end,
    acc, gu_acc, gu_send, gu_recv,
    s_sem, w_sem, t_sem,
    yz_send, yz_recv, fw_send, fw_recv, ag_send, ag_recv, pt_send, pt_recv,
    sib_send, sib_recv, ring_send, ring_recv,
):
    nx = n_dp // 2
    rows = n_dp * CAP
    slots = rows * n_e
    toks, width = tokens_hbm.shape
    chunk = width // nx
    half = chunk // 2
    acc_g, acc_u, acc_h = (acc.at[pl.ds(i * slots, slots)] for i in range(3))
    hid = w_down.shape[1]
    p = lax.axis_index("dp")
    e = lax.axis_index("expert")
    x = p // 2
    core = p % 2

    def at_x(d):
        return {"dp": lax.rem(x + d, nx) * 2 + core}

    sibling = {"dp": x * 2 + 1 - core}

    order = (2, 1, 3, 0)

    def away(j):
        if isinstance(j, int):
            return order[j]
        return jnp.where(j == 0, 2, jnp.where(j == 1, 1, jnp.where(j == 2, 3, 0)))

    def cols(j):
        return pl.ds(pl.multiple_of(lax.rem(x + away(j), nx) * chunk, chunk), chunk)

    small = [
        pltpu.make_async_copy(src, dst, s_sem.at[i])
        for i, (src, dst) in enumerate((
            (ids_hbm, ids_r), (rep_hbm, rep_r), (place_hbm, place_t),
            (count_hbm, count_ref), (prob_hbm, prob_r),
        ))
    ]
    for copy in small:
        copy.start()

    barrier = pltpu.get_barrier_semaphore()

    def greet(d, _):
        pl.semaphore_signal(
            barrier, inc=1, device_id={"expert": lax.rem(e + d, n_e)}, device_id_type=MESH
        )
        return 0

    lax.fori_loop(1, n_e, greet, 0)
    for d in range(1, nx):
        pl.semaphore_signal(barrier, inc=1, device_id=at_x(d), device_id_type=MESH)
    pl.semaphore_signal(barrier, inc=1, device_id=sibling, device_id_type=MESH)

    def load_gate(j):
        return pltpu.make_async_copy(w_gate.at[0, cols(j)], wg.at[j], w_sem.at[0, j])

    def load_up(j):
        return pltpu.make_async_copy(w_up.at[0, cols(j)], wu.at[j], w_sem.at[1, j])

    def load_down(j):
        return pltpu.make_async_copy(w_down.at[0, :, cols(j)], wd.at[j], w_sem.at[2, j])

    def load_tok(j):
        return pltpu.make_async_copy(tokens_hbm.at[:, cols(j)], tokens.at[j], t_sem.at[0, j])

    def load_cot(j):
        return pltpu.make_async_copy(d_out_hbm.at[:, cols(j)], d_out.at[j], t_sem.at[1, j])

    for j in range(nx):
        load_tok(j).start()
    for j in range(nx):
        load_cot(j).start()
        load_gate(j).start()
        load_up(j).start()
    for j in range(nx):
        load_down(j).start()

    for copy in small:
        copy.wait()
    count = count_ref[0].astype(F32)
    place = place_t[...].astype(F32).astype(BF)
    tgt_r, dst_r, exp_r = [], [], []
    for k in range(2):
        er = ids_r[k : k + 1, :].astype(F32)
        rr = rep_r[k : k + 1, :].astype(F32)
        of_expert = jnp.where(iota((n_e, toks), 0) == er, 1.0, 0.0).astype(BF)
        holders = dot_nn(place, of_expert)
        dr = jnp.sum(jnp.where(iota((n_dp, toks), 0) == rr, holders, 0.0), axis=0, keepdims=True)
        exp_r.append(er)
        dst_r.append(dr)
        tgt_r.append(dr * n_e + er)
    t_sub = iota((toks, toks), 0)
    t_lane = iota((toks, toks), 1)
    diagonal = t_sub == t_lane

    def as_column(row):
        return jnp.sum(jnp.where(diagonal, row, 0.0), axis=1, keepdims=True)

    tgt_c = [as_column(tgt_r[k]) for k in range(2)]
    before = (t_sub < t_lane) & (t_sub < count)
    slot_r = []
    for k in range(2):
        rank = jnp.zeros((1, toks), F32)
        for m in range(2):
            rank += jnp.sum(
                jnp.where((tgt_c[m] == tgt_r[k]) & before, 1.0, 0.0), axis=0, keepdims=True
            )
        keep = (rank < CAP) & (iota((1, toks), 1) < count)
        slot_r.append(jnp.where(keep, exp_r[k] * rows + dst_r[k] * CAP + rank, -1.0))
    slot_sub = iota((slots, toks), 0)
    slot_lane = iota((toks, slots), 1)
    hit0 = slot_sub == slot_r[0]
    hit1 = slot_sub == slot_r[1]
    sel[...] = jnp.where(hit0 | hit1, 1.0, 0.0).astype(BF)

    def rest_of_routing():
        wcol[...] = jnp.sum(
            jnp.where(hit0, prob_r[0:1, :], 0.0) + jnp.where(hit1, prob_r[1:2, :], 0.0),
            axis=1, keepdims=True,
        )
        pick0[...] = jnp.where(slot_lane == as_column(slot_r[0]), 1.0, 0.0).astype(BF)
        pick1[...] = jnp.where(slot_lane == as_column(slot_r[1]), 1.0, 0.0).astype(BF)
        prob_c[0] = as_column(prob_r[0:1, :])
        prob_c[1] = as_column(prob_r[1:2, :])

    side = 4

    def block(i):
        return pl.ds(pl.multiple_of(i * rows, rows), rows)

    def exchange(stage, src, dst, j):
        def one(d, _):
            q = lax.rem(e // side + d // side, side) * side + lax.rem(e % side + d % side, side)
            pltpu.make_async_remote_copy(
                src.at[j, block(q)], dst.at[j, block(e)],
                yz_send.at[stage, j], yz_recv.at[stage, j],
                device_id={"expert": q}, device_id_type=MESH,
            ).start()
            return 0

        lax.fori_loop(1, n_e, one, 0)
        pltpu.make_async_copy(
            src.at[j, block(e)], dst.at[j, block(e)], yz_recv.at[stage, j]
        ).start()

    def arrived(stage, dst, j):
        pltpu.make_async_copy(dst.at[j], dst.at[j], yz_recv.at[stage, j]).wait()

    def sent(stage, src, j):
        part = src.at[j, pl.ds(0, slots - rows)]
        pltpu.make_async_copy(part, part, yz_send.at[stage, j]).wait()

    def forward(j):
        return pltpu.make_async_remote_copy(
            x_recv.at[j], xs.at[j], fw_send.at[j], fw_recv.at[j],
            device_id=at_x(away(j)), device_id_type=MESH,
        )

    other = pl.multiple_of((1 - core) * half, half)
    mine = pl.multiple_of(core * half, half)

    def hidden_over():
        return pltpu.make_async_remote_copy(
            hs, h_sib, sib_send.at[nx], sib_recv.at[nx],
            device_id=sibling, device_id_type=MESH,
        )

    def cot_over(j):
        return pltpu.make_async_remote_copy(
            c_recv.at[j, :, pl.ds(other, half)], cot_sib.at[j], sib_send.at[j], sib_recv.at[j],
            device_id=sibling, device_id_type=MESH,
        )

    rcut = hid // 2

    def ring_half(way):
        r = pl.ds(way * rcut, rcut)
        return pltpu.make_async_remote_copy(
            r_send.at[0, r], r_mid.at[way], ring_send.at[way], ring_recv.at[way],
            device_id=at_x(1 if way == 0 else nx - 1), device_id_type=MESH,
        )

    def ring_whole(way):
        return pltpu.make_async_remote_copy(
            r_send.at[1 + way], r_end.at[way], ring_send.at[2 + way], ring_recv.at[2 + way],
            device_id=at_x(1 if way == 0 else nx - 1), device_id_type=MESH,
        )

    def down_part(j, start, size):
        c = pl.ds(start, size)
        m = pl.ds(pl.multiple_of(mine + start, size), size)
        return dot_tn(hs[...], c_recv[j, :, m]) + dot_tn(h_sib[...], cot_sib[j, :, c])

    cut = slots // 2

    def hand(which, buf, way):
        return pltpu.make_async_remote_copy(
            buf.at[0], buf.at[1 if way == 0 else nx - 1],
            ag_send.at[which, way], ag_recv.at[which, way],
            device_id=at_x(1 if way == 0 else nx - 1), device_id_type=MESH,
        )

    def relay(which, buf, way):
        r = pl.ds(way * cut, cut)
        return pltpu.make_async_remote_copy(
            buf.at[1 if way == 0 else nx - 1, r], buf.at[2, r],
            ag_send.at[which, 2 + way], ag_recv.at[which, 2 + way],
            device_id=at_x(1 if way == 0 else nx - 1), device_id_type=MESH,
        )

    def hand_out(which, buf):
        for way in (0, 1):
            hand(which, buf, way).start()

    def pass_on(which, buf):
        for way in (0, 1):
            hand(which, buf, way).wait_recv()
            relay(which, buf, way).start()

    def all_here(which, buf):
        for way in (0, 1):
            relay(which, buf, way).wait_recv()

    def gather_x(j):
        load_tok(j).wait()
        a_send[j] = dot_nn(sel[...], tokens[j]).astype(BF)

    gather_x(0)
    pl.semaphore_wait(barrier, n_e - 1 + nx - 1 + 1)
    exchange(0, a_send, x_recv, 0)

    def first(j, _):
        gather_x(j)

        @pl.when(j < 2)
        def _():
            exchange(0, a_send, x_recv, j)

        return 0

    lax.fori_loop(1, nx, first, 0)
    rest_of_routing()

    def gather_cot(j, _):
        load_cot(j).wait()
        raw = dot_nn(sel[...], d_out[j])
        b_send[j] = (raw * wcol[...]).astype(BF)
        return 0

    lax.fori_loop(0, nx, gather_cot, 0)

    acc_g[...] = jnp.zeros_like(acc_g)
    acc_u[...] = jnp.zeros_like(acc_u)
    acc_h[...] = jnp.zeros_like(acc_h)

    def pre_step(j, _):
        arrived(0, x_recv, j)

        @pl.when(j == 0)
        def _():
            for later in range(2, nx):
                exchange(0, a_send, x_recv, later)

        @pl.when(j > 0)
        def _():
            exchange(1, b_send, c_recv, j - 1)

        @pl.when(j == nx - 1)
        def _():
            exchange(1, b_send, c_recv, j)


        @pl.when(j < nx - 1)
        def _():
            forward(j).start()

        load_gate(j).wait()
        load_up(j).wait()
        acc_g[...] += dot_nn(x_recv[j], wg[j])
        acc_u[...] += dot_nn(x_recv[j], wu[j])
        return 0

    lax.fori_loop(0, nx, pre_step, 0)

    band = min(32, slots)

    def activate(i, _):
        r = pl.ds(pl.multiple_of(i * band, band), band)
        pre_g = acc_g[r, :]
        pre_u = acc_u[r, :]
        sig = jax.nn.sigmoid(pre_g)
        val = pre_g * sig
        hs[r, :] = (val * pre_u).astype(BF)
        acc_g[r, :] = pre_u * (sig * (1.0 + pre_g * (1.0 - sig)))
        acc_u[r, :] = val
        return 0

    lax.fori_loop(0, slots // band, activate, 0)
    hidden_over().start()

    tile = half // 2
    tiles = [(t * tile, pl.ds(t * tile, tile)) for t in range(half // tile)]

    def cot_step(j, _):
        arrived(1, c_recv, j)
        cot_over(j).start()
        load_down(j).wait()
        sent(0, a_send, j)
        a_send[j] = dot_nn(hs[...], wd[j]).astype(BF)
        exchange(2, a_send, o_recv, j)
        acc_h[...] += dot_nt(c_recv[j], wd[j])
        return 0

    cot_step(0, 0)
    hidden_over().wait_recv()
    cot_over(0).wait_recv()
    for start, r in tiles:
        r_send[0, :, r] = down_part(0, start, tile).astype(BF)
    for way in (0, 1):
        ring_half(way).start()
    cot_step(1, 0)
    cot_step(2, 0)
    for way in (0, 1):
        cot_over(1 + way).wait_recv()
        ring_half(way).wait_recv()
        part = pl.ds(way * rcut, rcut)
        rest = pl.ds((1 - way) * rcut, rcut)
        for start, r in tiles:
            value = down_part(1 + way, start, tile)
            with_mid = value[way * rcut : (way + 1) * rcut] + r_mid[way, :, r].astype(F32)
            r_send[1 + way, part, r] = with_mid.astype(BF)
            r_send[1 + way, rest, r] = value[(1 - way) * rcut : (2 - way) * rcut].astype(BF)
        ring_whole(way).start()
    arrived(1, c_recv, nx - 1)
    load_down(nx - 1).wait()
    acc_h[...] += dot_nt(c_recv[nx - 1], wd[nx - 1])

    def slopes(i, _):
        r = pl.ds(pl.multiple_of(i * band, band), band)
        d_h = acc_h[r, :]
        gs[0, r, :] = (d_h * acc_g[r, :]).astype(BF)
        us[0, r, :] = (d_h * acc_u[r, :]).astype(BF)
        return 0

    lax.fori_loop(0, slots // band, slopes, 0)
    hand_out(0, gs)
    hand_out(1, us)
    cot_over(nx - 1).start()
    sent(0, a_send, nx - 1)
    a_send[nx - 1] = dot_nn(hs[...], wd[nx - 1]).astype(BF)
    exchange(2, a_send, o_recv, nx - 1)

    def dx_step(j, _):
        sent(1, b_send, j)
        b_send[j] = (dot_nt(gs[0], wg[j]) + dot_nt(us[0], wu[j])).astype(BF)
        exchange(3, b_send, d_recv, j)
        return 0

    lax.fori_loop(0, nx, dx_step, 0)

    def out_step(j, carry):
        g0, g1 = carry
        arrived(2, o_recv, j)
        got = o_recv[j]
        out0 = dot_nn(pick0[...], got)
        out1 = dot_nn(pick1[...], got)
        cot = d_out[j].astype(F32)
        layer_out[:, cols(j)] = (prob_c[0] * out0 + prob_c[1] * out1).astype(BF)
        g0 = g0 + jnp.sum(cot * out0, axis=1, keepdims=True)
        g1 = g1 + jnp.sum(cot * out1, axis=1, keepdims=True)
        return g0, g1

    zero = jnp.zeros((toks, 1), F32)
    carry = lax.fori_loop(0, nx - 2, out_step, (zero, zero))
    pass_on(0, gs)
    carry = out_step(nx - 2, carry)
    pass_on(1, us)
    g0, g1 = out_step(nx - 1, carry)

    def as_row(column):
        return jnp.sum(jnp.where(diagonal, column, 0.0), axis=0, keepdims=True)

    d_gates[0:1, :] = as_row(g0)
    d_gates[1:2, :] = as_row(g1)

    def row_block(d):
        if d == 0:
            return x_recv.at[nx - 1]
        return xs.at[order.index(d)]

    def grad_tile(which, start, blocks):
        c = pl.ds(pl.multiple_of(start, tile), tile)
        total = None
        for d in blocks:
            term = dot_tn(row_block(d)[:, c], (gs, us)[which][d])
            total = term if total is None else total + term
        return total

    def part_copy(which):
        return pltpu.make_async_remote_copy(
            gu_send.at[which], gu_recv.at[which], pt_send.at[which], pt_recv.at[which],
            device_id=sibling, device_id_type=MESH,
        )

    near_blocks = [0, 1, nx - 1]

    def first_blocks(which):
        for start, r in tiles:
            gu_acc[which, 0, r, :] = grad_tile(which, other + start, near_blocks)
            gu_acc[which, 1, r, :] = grad_tile(which, mine + start, near_blocks)

    def last_block(which):
        all_here(which, (gs, us)[which])
        for start, r in tiles:
            last = grad_tile(which, other + start, [2])
            gu_send[which, r, :] = (gu_acc[which, 0, r, :] + last).astype(BF)
        part_copy(which).start()
        for start, r in tiles:
            gu_acc[which, 1, r, :] += grad_tile(which, mine + start, [2])

    def finish(which):
        part_copy(which).wait_recv()
        (g_gate, g_up)[which][0] = (
            gu_acc[which, 1] + gu_recv[which].astype(F32)
        ).astype(BF)

    def finish_down():
        for way in (0, 1):
            ring_whole(way).wait_recv()
        cot_over(nx - 1).wait_recv()
        for start, r in tiles:
            value = down_part(nx - 1, start, tile)
            value += r_end[0, :, r].astype(F32) + r_end[1, :, r].astype(F32)
            g_down[0, :, r] = value.astype(BF)

    def tok_step(j):
        arrived(3, d_recv, j)
        d_tokens[:, cols(j)] = dot_nn(pick0[...] + pick1[...], d_recv[j]).astype(BF)

    for j in range(nx - 1):
        forward(j).wait_recv()
    first_blocks(0)
    first_blocks(1)
    finish_down()
    tok_step(0)
    last_block(0)
    tok_step(1)
    last_block(1)
    finish(0)
    tok_step(2)
    finish(1)
    tok_step(3)

    for which in (0, 1):
        part_copy(which).wait_send()

    def drain(j, _):
        sent(2, a_send, j)
        sent(3, b_send, j)
        return 0

    lax.fori_loop(0, nx, drain, 0)
    for j in range(nx - 1):
        forward(j).wait_send()
    for j in range(nx):
        cot_over(j).wait_send()
    hidden_over().wait_send()
    for way in (0, 1):
        ring_half(way).wait_send()
        ring_whole(way).wait_send()
    for which, buf in enumerate((gs, us)):
        for way in (0, 1):
            hand(which, buf, way).wait_send()
            relay(which, buf, way).wait_send()


def place_kernel(*refs):
    n = (len(refs) - 1) // 2
    copies = [pltpu.make_async_copy(refs[i], refs[n + i], refs[-1].at[i]) for i in range(n)]
    for copy in copies:
        copy.start()
    for copy in copies:
        copy.wait()


def on_device(
    tokens, gate_probs, expert_ids, placement, replica, row_counts, w_gate, w_up, w_down, d_out
):
    n_dp = lax.axis_size("dp")
    n_e = lax.axis_size("expert")
    nx = n_dp // 2
    toks, width = tokens.shape
    hid = w_gate.shape[2]
    slots = n_dp * CAP * n_e
    chunk = width // nx
    half = chunk // 2
    vmem = pl.BlockSpec(memory_space=pltpu.VMEM)
    hbm = pl.BlockSpec(memory_space=pl.ANY)
    yz = (nx, slots, chunk)
    near = (nx - 1, slots, chunk)
    wide = (nx, slots, hid)
    dma = pltpu.SemaphoreType.DMA
    flops = 18 * slots * width * hid
    outs = (
        jax.ShapeDtypeStruct((toks, width), BF),
        jax.ShapeDtypeStruct((toks, width), BF),
        jax.ShapeDtypeStruct((2, toks), F32),
        jax.ShapeDtypeStruct((1, half, hid), BF),
        jax.ShapeDtypeStruct((1, half, hid), BF),
        jax.ShapeDtypeStruct((1, hid, half), BF),
    )
    mine = (nx, toks, chunk)
    results = pl.pallas_call(
        functools.partial(moe_kernel, n_dp, n_e),
        out_shape=[pltpu.VMEM(out.shape, out.dtype) for out in outs],
        in_specs=[hbm] * 10,
        out_specs=[vmem] * 6,
        scratch_shapes=[
            pltpu.SMEM((1,), jnp.int32),
            pltpu.VMEM((2, toks), jnp.int32),
            pltpu.VMEM((2, toks), jnp.int32),
            pltpu.VMEM((2, toks), F32),
            pltpu.VMEM((n_dp, n_e), jnp.int32),
            pltpu.VMEM(mine, BF),
            pltpu.VMEM(mine, BF),
            pltpu.VMEM((slots, toks), BF),
            pltpu.VMEM((toks, slots), BF),
            pltpu.VMEM((toks, slots), BF),
            pltpu.VMEM((slots, 1), F32),
            pltpu.VMEM((2, toks, 1), F32),
            pltpu.VMEM((nx, chunk, hid), BF),
            pltpu.VMEM((nx, chunk, hid), BF),
            pltpu.VMEM((nx, hid, chunk), BF),
            pltpu.VMEM(yz, BF),
            pltpu.VMEM(yz, BF),
            pltpu.VMEM(yz, BF),
            pltpu.VMEM(yz, BF),
            pltpu.VMEM(yz, BF),
            pltpu.VMEM(yz, BF),
            pltpu.VMEM(near, BF),
            pltpu.VMEM((nx, slots, half), BF),
            pltpu.VMEM((slots, hid), BF),
            pltpu.VMEM((slots, hid), BF),
            pltpu.VMEM(wide, BF),
            pltpu.VMEM(wide, BF),
            pltpu.VMEM((3, hid, half), BF),
            pltpu.VMEM((2, hid // 2, half), BF),
            pltpu.VMEM((2, hid, half), BF),
            pltpu.VMEM((3 * slots, hid), F32),
            pltpu.VMEM((2, 2, half, hid), F32),
            pltpu.VMEM((2, half, hid), BF),
            pltpu.VMEM((2, half, hid), BF),
            dma((5,)),
            dma((3, nx)),
            dma((2, nx)),
            dma((4, nx)),
            dma((4, nx)),
            dma((nx - 1,)),
            dma((nx - 1,)),
            dma((2, 4)),
            dma((2, 4)),
            dma((2,)),
            dma((2,)),
            dma((nx + 1,)),
            dma((nx + 1,)),
            dma((4,)),
            dma((4,)),
        ],
        compiler_params=pltpu.CompilerParams(
            collective_id=0, has_side_effects=True, vmem_limit_bytes=58 << 20
        ),
        cost_estimate=pl.CostEstimate(flops=flops, bytes_accessed=6 * width * hid, transcendentals=0),
        name="moe",
    )(
        row_counts, expert_ids.T, replica.T, gate_probs.T, placement.T,
        tokens, d_out, w_gate, w_up, w_down,
    )
    results = pl.pallas_call(
        place_kernel,
        out_shape=outs,
        in_specs=[hbm] * 6,
        out_specs=[hbm] * 6,
        scratch_shapes=[dma((6,))],
        compiler_params=pltpu.CompilerParams(vmem_limit_bytes=1 << 20),
        name="place",
    )(*[pltpu.with_memory_space_constraint(result, pltpu.VMEM) for result in results])
    layer_out, d_tokens, d_gates, g_gate, g_up, g_down = results
    return layer_out, d_tokens, d_gates.T, g_gate, g_up, g_down


def solution(mesh):
    rows = P(("dp", "expert"), None)
    weight = P("expert", None, None)
    return jax.shard_map(
        on_device,
        mesh=mesh,
        in_specs=(
            rows, rows, rows, P(), rows, P(("dp", "expert")), weight, weight, weight, rows,
        ),
        out_specs=(
            rows, rows, rows,
            P("expert", "dp", None), P("expert", "dp", None), P("expert", None, "dp"),
        ),
        check_vma=False,
    )
```
